32 devices in a mesh: dp: 16 (over z, y, core), basis: 2 (over x).
Axes of the slice: x: 2, y: 2, z: 4, core: 2. Of those that a mesh axis runs over, the one named last changes fastest.
Arguments:
- tokens: bfloat16 [32, 640, 768], P(('dp', 'basis')), may hold values from -6 to 6
- w_qkv: bfloat16 [768, 2304], replicated, may hold values from -0.21875 to 0.21875
- w_out: bfloat16 [768, 768], replicated, may hold values from -0.875 to 0.875
- w_up: bfloat16 [768, 3072], replicated, may hold values from -0.21875 to 0.21875
- w_down: bfloat16 [3072, 768], replicated, may hold values from -0.109375 to 0.109375
- gain_one: float32 [768], replicated, may hold values from 0.5 to 1.5
- shift_one: float32 [768], replicated, may hold values from -3 to 3
- gain_two: float32 [768], replicated, may hold values from 0.5 to 1.5
- shift_two: float32 [768], replicated, may hold values from -3 to 3
- coeffs: bfloat16 [32, 256, 768], P('dp', 'basis'), may hold values from -6 to 6
- flags: int32 [32], P(('dp', 'basis')), may hold values 0 or 1
- centres: int32 [32, 12, 2], P('dp'), may hold values from 0 to 255
- widths: int32 [32, 12, 2], P('dp'), may hold values from 1 to 8
- cotangent: bfloat16 [32, 640, 768], P(('dp', 'basis')), may hold values from -6 to 6
Outputs:
- mixed: bfloat16 [32, 640, 768], P(('dp', 'basis'))
- grad_tokens: float32 [32, 640, 768], P(('dp', 'basis'))
- grad_coeffs: float32 [32, 256, 768], P('dp', 'basis')
- grad_w_qkv: float32 [768, 2304], P(('dp', 'basis'))
- grad_w_out: float32 [768, 768], P(('dp', 'basis'))
- grad_w_up: float32 [768, 3072], P(('dp', 'basis'))
- grad_w_down: float32 [3072, 768], P(('dp', 'basis'))
- grad_gain_one: float32 [768], P(('dp', 'basis'))
- grad_shift_one: float32 [768], P(('dp', 'basis'))
- grad_gain_two: float32 [768], P(('dp', 'basis'))
- grad_shift_two: float32 [768], P(('dp', 'basis'))
The draws below stay inside these ranges and needn't reach their ends.
Inputs may be any that keep to these rules, and one draw needn't show every extreme that they name: `flags`: 1 where a sequence carries memory coefficients, 0 where its memory is empty.
All inputs are finite; a program needn't handle non-finite values. No bound on the sum of `flags` on one device may be relied on, other than what follows from the above.
Results may differ from the reference program's by a relative error of at most 0.014.
Values may be sent and summed in bfloat16 or wider, within the bound.
A program may use at most 256 MiB of HBM per device.

```python
import math
import jax
import jax.numpy as jnp
from jax import lax

D = 768
H = 12
HD = 64
FF = 3072
NB = 256
SEQ_LEN = 640
QBLK = 320
NQB = 2
SEQS = 32


def place_ends(entries, own_key, least, high):
    longest = entries.shape.index(max(entries.shape))
    spots = []
    for shift in (0, 1):
        where = [jax.random.randint(jax.random.fold_in(own_key, axis), (), 0, length) for axis, length in enumerate(entries.shape)]
        where[longest] = (where[longest] + shift) % entries.shape[longest]
        spots.append(tuple(where))
    return entries.at[spots[0]].set(least).at[spots[1]].set(high)


def block_levels(own_key, extent, pieces, smallest, largest):
    level = 1.0
    for axis_at, parts in pieces:
        steps = jax.random.uniform(jax.random.fold_in(jax.random.fold_in(own_key, 6), axis_at), (parts,), jnp.float32, smallest / len(pieces), largest / len(pieces))
        level = level * jnp.repeat(jnp.exp(steps), extent[axis_at] // parts).reshape((-1,) + (1,) * (len(extent) - 1 - axis_at))
    return level


def noise(key, shape, scale, most, cuts=(), kind=jnp.bfloat16):
    drawn = jax.random.normal(key, shape, jnp.float32) * scale
    if len(cuts) > 0:
        drawn = block_levels(key, shape, cuts, -0.22, 0.18) * drawn
    return jnp.clip(drawn, min=-most, max=most).astype(kind)


def setup_inputs(seed: int = 0) -> dict:
    streams_of = jax.random.split(jax.random.key(seed), 15)
    tokens = noise(streams_of[0], (SEQS, SEQ_LEN, D), 1.0, 6.0, ((0, 32),))
    w_qkv = noise(streams_of[1], (D, 3 * D), D ** -0.5, 0.21875)
    w_out = noise(streams_of[2], (D, D), (D // 16) ** -0.5, 0.875)
    w_up = noise(streams_of[3], (D, FF), D ** -0.5, 0.21875)
    w_down = noise(streams_of[4], (FF, D), FF ** -0.5, 0.109375)
    gain_one = jnp.clip(1.0 + 0.1 * jax.random.normal(streams_of[5], (D,), jnp.float32), 0.5, 1.5)
    shift_one = noise(streams_of[6], (D,), 0.5, 3.0, (), jnp.float32)
    gain_two = jnp.clip(1.0 + 0.1 * jax.random.normal(streams_of[7], (D,), jnp.float32), 0.5, 1.5)
    shift_two = noise(streams_of[8], (D,), 0.5, 3.0, (), jnp.float32)
    coeffs = noise(streams_of[9], (SEQS, NB, D), 1.0, 6.0, ((0, 16), (1, 2)))
    flags = place_ends((jax.random.randint(streams_of[10], (SEQS,), 0, 2) < 1).astype(jnp.int32), jax.random.fold_in(streams_of[10], 1), 0, 1)
    centres = place_ends(jax.random.randint(streams_of[11], (SEQS, H, NQB), 0, NB), jax.random.fold_in(streams_of[11], 1), 0, NB - 1).astype(jnp.int32)
    widths = place_ends(jax.random.randint(streams_of[12], (SEQS, H, NQB), 1, 9), jax.random.fold_in(streams_of[12], 1), 1, 8).astype(jnp.int32)
    cotangent = noise(streams_of[13], (SEQS, SEQ_LEN, D), 1.0, 6.0, ((0, 32),))
    return dict(tokens=tokens, w_qkv=w_qkv, w_out=w_out, w_up=w_up, w_down=w_down, gain_one=gain_one, shift_one=shift_one, gain_two=gain_two, shift_two=shift_two, coeffs=coeffs, flags=flags, centres=centres, widths=widths, cotangent=cotangent)


@jax.custom_vjp
def low(v):
    return lax.optimization_barrier(v.astype(jnp.bfloat16)).astype(jnp.float32)

@jax.custom_vjp
def low_back(v):
    return v

def low_keep(v):
    return (low(v), None)

def low_pass(kept, grad):
    return (grad,)

def back_keep(v):
    return (v, None)

def back_low(kept, grad):
    return (low(grad),)
low.defvjp(low_keep, low_pass)
low_back.defvjp(back_keep, back_low)
eps = 1e-05
highest = lax.Precision.HIGHEST

def layer_norm(values, gain, shift):
    centred = values - lax.optimization_barrier(jnp.mean(values, axis=-1, keepdims=True))
    inverse = lax.rsqrt(lax.optimization_barrier(jnp.mean(centred * centred, axis=-1, keepdims=True)) + eps)
    return centred * inverse * gain + shift

def basis_weights(centres, widths, rows):
    spread = (widths * widths).astype(jnp.float32) + 4.0
    gap = centres[..., None].astype(jnp.float32) - rows.astype(jnp.float32)
    return 2.0 * lax.rsqrt(spread)[..., None] * jnp.exp(-gap * gap / (2.0 * spread[..., None]))

def layer(tokens, coeffs, w_qkv, w_out, w_up, w_down, gain_one, shift_one, gain_two, shift_two, flag_values, weights_e):
    group, seq_len, width = tokens.shape
    scale = 1.0 / math.sqrt(HD)
    hidden_one = low(layer_norm(tokens, gain_one, shift_one))
    qkv = low(low_back(jnp.matmul(hidden_one, w_qkv, precision=highest))).reshape(group, seq_len, 3, H, HD)
    query, key, value = (qkv[:, :, 0], qkv[:, :, 1], qkv[:, :, 2])
    scores = low_back(jnp.einsum('gqhe,gkhe->ghqk', query, key, precision=highest) * scale)
    row_ids = jnp.arange(seq_len, dtype=jnp.int32)[:, None]
    col_ids = jnp.arange(seq_len, dtype=jnp.int32)[None, :]
    scores = jnp.where(col_ids <= row_ids, scores, -1e+30)
    probs = low(jax.nn.softmax(scores, axis=-1))
    local = jnp.einsum('ghqk,gkhe->gqhe', probs, value, precision=highest)
    memory = low(low_back(jnp.einsum('ghbj,gjd->ghbd', weights_e, coeffs, precision=highest)))
    w_kv = w_qkv[:, D:].reshape(D, 2, H, HD)
    mem_kv = low(low_back(jnp.einsum('ghbd,dche->gchbe', memory, w_kv, precision=highest)))
    mem_key, mem_value = (mem_kv[:, 0], mem_kv[:, 1])
    query_blocks = query.reshape(group, NQB, QBLK, H, HD)
    mem_score = jnp.einsum('gbthe,ghbe->gbth', query_blocks, mem_key, precision=highest) * scale
    gate = jax.nn.sigmoid(mem_score) * flag_values[:, None, None, None]
    long_term = gate[..., None] * jnp.transpose(mem_value, (0, 2, 1, 3))[:, :, None]
    attended = local + long_term.reshape(group, seq_len, H, HD)
    joined = low(low_back(attended.reshape(group, seq_len, width)))
    after = tokens + low_back(jnp.matmul(joined, w_out, precision=highest))
    hidden_two = low(layer_norm(after, gain_two, shift_two))
    pre = low_back(jnp.matmul(hidden_two, w_up, precision=highest))
    act = low(jax.nn.gelu(pre, approximate=True))
    return after + low_back(jnp.matmul(act, w_down, precision=highest))

def reference(tokens, w_qkv, w_out, w_up, w_down, gain_one, shift_one, gain_two, shift_two, coeffs, flags, centres, widths, cotangent):
    group = math.gcd(SEQS, max(1, 4096 // SEQ_LEN))
    count = SEQS // group

    def split(values):
        return values.reshape((count, group) + values.shape[1:])
    params = (w_qkv.astype(jnp.float32), w_out.astype(jnp.float32), w_up.astype(jnp.float32), w_down.astype(jnp.float32), gain_one, shift_one, gain_two, shift_two)
    rows = jnp.arange(NB, dtype=jnp.int32)

    def one_group(totals, items):
        tok, coef, flag, centre, spread, cot = items
        weights_e = low(basis_weights(centre, spread, rows))
        flag_values = flag.astype(jnp.float32)

        def forward(tok_f, coef_f, *weights):
            return layer(tok_f, coef_f, *weights, flag_values, weights_e)
        result, pullback = jax.vjp(forward, tok.astype(jnp.float32), coef.astype(jnp.float32), *params)
        grads = pullback(cot.astype(jnp.float32))
        totals = tuple((total + grad for total, grad in zip(totals, grads[2:])))
        return (totals, (result.astype(jnp.bfloat16), grads[0], grads[1]))
    zeros = tuple((jnp.zeros_like(param) for param in params))
    totals, outputs = lax.scan(one_group, zeros, (split(tokens), split(coeffs), split(flags), split(centres), split(widths), split(cotangent)))
    mixed = outputs[0].reshape(SEQS, SEQ_LEN, D)
    grad_tokens = outputs[1].reshape(SEQS, SEQ_LEN, D)
    grad_coeffs = outputs[2].reshape(SEQS, NB, D)
    return (mixed, grad_tokens, grad_coeffs, totals[0], totals[1], totals[2], totals[3], totals[4], totals[5], totals[6], totals[7])
```

```python
import functools
import math

import jax
import jax.numpy as jnp
from jax import lax
from jax.experimental import pallas as pl
from jax.experimental.pallas import tpu as pltpu
from jax.sharding import PartitionSpec as P

eps = 1e-05
f32 = jnp.float32
bf16 = jnp.bfloat16
MESH = pl.DeviceIdType.MESH
CUT = 32
STAGES = 5


def norm_parts(values, gain, shift):
    centred = values - jnp.mean(values, axis=-1, keepdims=True)
    inverse = lax.rsqrt(jnp.mean(centred * centred, axis=-1, keepdims=True) + eps)
    normed = centred * inverse
    return (normed * gain + shift, normed, inverse)


def norm_back(upstream, normed, inverse, gain):
    scaled = upstream * gain
    inner = (
        scaled
        - jnp.mean(scaled, axis=-1, keepdims=True)
        - normed * jnp.mean(scaled * normed, axis=-1, keepdims=True)
    )
    return (inverse * inner, jnp.sum(upstream * normed, axis=0), jnp.sum(upstream, axis=0))


def basis_weights(centres, widths, rows):
    spread = (widths * widths).astype(jnp.float32) + 4.0
    gap = centres[..., None].astype(jnp.float32) - rows.astype(jnp.float32)
    return 2.0 * lax.rsqrt(spread)[..., None] * jnp.exp(-gap * gap / (2.0 * spread[..., None]))


def causal_scores(query_part, key_part, first, scale):
    scores = (
        jnp.einsum("qhe,khe->hqk", query_part, key_part, preferred_element_type=jnp.float32) * scale
    )
    row_ids = first + jnp.arange(query_part.shape[0], dtype=jnp.int32)[:, None]
    col_ids = jnp.arange(key_part.shape[0], dtype=jnp.int32)[None, :]
    return jnp.where(col_ids <= row_ids, scores, -1e30)


class Place:
    def __init__(self, mesh_shape):
        self.dp, self.basis = mesh_shape["dp"], mesh_shape["basis"]
        self.bits = (self.dp * self.basis).bit_length() - 1
        self.low = self.bits - STAGES
        self.basis_bits = self.basis.bit_length() - 1

    def here(self):
        self.me_dp, self.me_basis = lax.axis_index("dp"), lax.axis_index("basis")
        flat = self.me_dp * self.basis + self.me_basis
        self.mine = [lax.rem(flat // (1 << (self.low + b)), 2) for b in range(STAGES)]

    def partner(self, b):
        flip = 1 - 2 * self.mine[b]
        bit = self.low + b
        if bit < self.basis_bits:
            return (self.me_dp, self.me_basis + flip * (1 << bit))
        return (self.me_dp + flip * (1 << (bit - self.basis_bits)), self.me_basis)

    def spot(self, block, order):
        where = 0
        for stage, b in enumerate(order):
            bit = (block >> b) & 1
            differs = 1 - self.mine[b] if bit else self.mine[b]
            where = where + differs * (1 << (STAGES - 1 - stage))
        return where


class Share:
    def __init__(self, place, order, own, recv, send_sem, recv_sem):
        self.place, self.order, self.own, self.recv = place, order, own, recv
        self.send_sem, self.recv_sem = send_sem, recv_sem
        self.flying = {}

    def send(self, stage):
        count = CUT >> (stage + 1)
        copy = pltpu.make_async_remote_copy(
            src_ref=self.own.at[pl.ds(count, count)],
            dst_ref=self.recv.at[pl.ds(CUT - 2 * count, count)],
            send_sem=self.send_sem.at[stage],
            recv_sem=self.recv_sem.at[stage],
            device_id=self.place.partner(self.order[stage]),
            device_id_type=MESH,
        )
        copy.start()
        self.flying[stage] = copy

    def take(self, stage):
        count = CUT >> (stage + 1)
        self.flying[stage].wait()
        if stage == STAGES - 1:
            return
        first = CUT - 2 * count

        def add(k, carry):
            self.own[k] = self.own[k] + self.recv[first + k]
            return carry

        lax.fori_loop(0, count, add, 0)

    def last(self):
        return self.own[0].astype(f32) + self.recv[CUT - 2].astype(f32)


class Whole:
    def __init__(self, place, own, recv, send_sem, recv_sem):
        self.place, self.own, self.recv = place, own, recv
        self.send_sem, self.recv_sem = send_sem, recv_sem
        self.flying = {}

    def send(self, stage):
        copy = pltpu.make_async_remote_copy(
            src_ref=self.own.at[stage],
            dst_ref=self.recv.at[stage],
            send_sem=self.send_sem.at[stage],
            recv_sem=self.recv_sem.at[stage],
            device_id=self.place.partner(stage),
            device_id_type=MESH,
        )
        copy.start()
        self.flying[stage] = copy

    def take(self, stage):
        self.flying[stage].wait()
        self.own[stage + 1] = self.own[stage] + self.recv[stage]


def greet(place):
    barrier = pltpu.get_barrier_semaphore()
    for b in range(STAGES):
        pl.semaphore_signal(barrier, inc=1, device_id=place.partner(b), device_id_type=MESH)
    pl.semaphore_wait(barrier, STAGES)


ORDERS = ((1, 0, 2, 3, 4), (1, 2, 3, 0, 4), (1, 3, 0, 2, 4))


def sum_kernel(place, count, *refs):
    given, small_in = refs[:count], refs[count]
    outs, small_out = refs[count + 1 : 2 * count + 1], refs[2 * count + 1]
    rest = list(refs[2 * count + 2 :])
    owns, recvs = rest[:count], rest[count : 2 * count]
    small_own, small_recv, load_sem, send_sem, recv_sem = rest[2 * count :]
    place.here()
    shares = [
        Share(place, ORDERS[i % 3], owns[i], recvs[i], send_sem.at[i], recv_sem.at[i])
        for i in range(count)
    ]
    small = Whole(place, small_own, small_recv, send_sem.at[count], recv_sem.at[count])
    for i, share in enumerate(shares):
        for block in range(CUT):
            pltpu.make_async_copy(
                given[i].at[block], owns[i].at[place.spot(block, share.order)], load_sem.at[i]
            ).start()
    small_own[0] = small_in[...]
    greet(place)
    for i, share in enumerate(shares):
        pltpu.make_async_copy(given[i], owns[i], load_sem.at[i]).wait()
        share.send(0)
    small.send(0)
    for stage in range(STAGES):
        for share in shares:
            share.take(stage)
            if stage < STAGES - 1:
                share.send(stage + 1)
        small.take(stage)
        if stage < STAGES - 1:
            small.send(stage + 1)
    for out, share in zip(outs, shares):
        out[...] = share.last()
    small_out[...] = small_own[STAGES]


def summed_shares(place, arrays, small):
    count = len(arrays)
    block = [(a.shape[1], a.shape[2]) for a in arrays]
    vm = pl.BlockSpec(memory_space=pltpu.VMEM)
    return pl.pallas_call(
        lambda *refs: sum_kernel(place, count, *refs),
        out_shape=[jax.ShapeDtypeStruct(b, f32) for b in block]
        + [jax.ShapeDtypeStruct(small.shape, f32)],
        in_specs=[pl.BlockSpec(memory_space=pl.ANY)] * count + [vm],
        out_specs=[vm] * (count + 1),
        scratch_shapes=[pltpu.VMEM((CUT,) + b, bf16) for b in block]
        + [pltpu.VMEM((CUT - 1,) + b, bf16) for b in block]
        + [
            pltpu.VMEM((STAGES + 1,) + small.shape, f32),
            pltpu.VMEM((STAGES,) + small.shape, f32),
            pltpu.SemaphoreType.DMA((count,)),
            pltpu.SemaphoreType.DMA((count + 1, STAGES)),
            pltpu.SemaphoreType.DMA((count + 1, STAGES)),
        ],
        compiler_params=pltpu.CompilerParams(
            collective_id=0, has_side_effects=True, vmem_limit_bytes=56 * 2**20
        ),
    )(*arrays, small)


def halve_rest(place, rows):
    for bit in reversed(range(place.low)):
        half = rows.shape[0] // 2
        if bit < place.basis_bits:
            axis, size, mask = "basis", place.basis, 1 << bit
        else:
            axis, size, mask = "dp", place.dp, 1 << (bit - place.basis_bits)
        mine = (lax.axis_index(axis) // mask) % 2
        keep = lax.dynamic_slice_in_dim(rows, mine * half, half, 0)
        give = lax.dynamic_slice_in_dim(rows, (1 - mine) * half, half, 0)
        rows = keep + lax.ppermute(give, axis, [(i, i ^ mask) for i in range(size)])
    return rows


def sum_rest(place, values):
    for bit in range(place.low):
        if bit < place.basis_bits:
            axis, size, mask = "basis", place.basis, 1 << bit
        else:
            axis, size, mask = "dp", place.dp, 1 << (bit - place.basis_bits)
        values = values + lax.ppermute(values, axis, [(i, i ^ mask) for i in range(size)])
    return values


def fold(grad, pieces):
    rows, columns = grad.shape
    split = grad.reshape(CUT, rows // CUT, pieces, columns // pieces)
    return jnp.transpose(split, (0, 2, 1, 3)).reshape(CUT, pieces * rows // CUT, columns // pieces)


def unfold(block, pieces):
    rows, columns = block.shape
    split = block.reshape(pieces, rows // pieces, columns)
    return jnp.transpose(split, (1, 0, 2)).reshape(rows // pieces, pieces * columns)


def on_device(
    place,
    tokens,
    w_qkv,
    w_out,
    w_up,
    w_down,
    gain_one,
    shift_one,
    gain_two,
    shift_two,
    coeffs,
    flags,
    centres,
    widths,
    cotangent,
):
    seq_len, width = (tokens.shape[1], tokens.shape[2])
    heads, blocks = (centres.shape[1], centres.shape[2])
    head_dim = width // heads
    span = seq_len // blocks
    scale = 1.0 / math.sqrt(head_dim)
    local_rows = coeffs.shape[1]
    step = min(512, seq_len)
    starts = list(range(0, seq_len, step))
    resid = tokens[0].astype(jnp.float32)
    normed_in, normed_one, inverse_one = norm_parts(resid, gain_one, shift_one)
    hidden_one = normed_in.astype(jnp.bfloat16)
    qkv = jnp.dot(hidden_one, w_qkv, preferred_element_type=jnp.float32).astype(jnp.bfloat16)
    qkv = qkv.reshape(seq_len, 3, heads, head_dim)
    query, key, value = (qkv[:, 0], qkv[:, 1], qkv[:, 2])
    rows = lax.axis_index("basis") * local_rows + jnp.arange(local_rows, dtype=jnp.int32)
    weights_e = basis_weights(centres, widths, rows).astype(jnp.bfloat16)
    partial_mem = jnp.einsum(
        "shbj,sjd->shbd", weights_e, coeffs, preferred_element_type=jnp.float32
    )
    summed = lax.psum_scatter(
        partial_mem.astype(jnp.bfloat16), "basis", scatter_dimension=0, tiled=True
    ).astype(jnp.float32)
    memory = summed[0].astype(jnp.bfloat16)
    local_parts = []
    log_totals = []
    for first in starts:
        finish = min(first + step, seq_len)
        scores = causal_scores(query[first:finish], key[:finish], first, scale)
        peak = jnp.max(scores, axis=-1, keepdims=True)
        expo = jnp.exp(scores - peak)
        total = jnp.sum(expo, axis=-1, keepdims=True)
        probs = (expo / total).astype(jnp.bfloat16)
        log_totals.append(peak + jnp.log(total))
        local_parts.append(
            jnp.einsum("hqk,khe->qhe", probs, value[:finish], preferred_element_type=jnp.float32)
        )
    local = jnp.concatenate(local_parts, axis=0)
    w_kv = w_qkv[:, width:].reshape(width, 2, heads, head_dim)
    mem_kv = jnp.einsum("hbd,dche->chbe", memory, w_kv, preferred_element_type=jnp.float32).astype(
        jnp.bfloat16
    )
    mem_key, mem_value = (mem_kv[0], mem_kv[1])
    flag = flags[0].astype(jnp.float32)
    query_blocks = query.reshape(blocks, span, heads, head_dim)
    mem_score = (
        jnp.einsum("bthe,hbe->bth", query_blocks, mem_key, preferred_element_type=jnp.float32)
        * scale
    )
    sigma = jax.nn.sigmoid(mem_score)
    gate = sigma * flag
    long_term = gate[..., None] * jnp.transpose(mem_value, (1, 0, 2))[:, None].astype(jnp.float32)
    attended = local + long_term.reshape(seq_len, heads, head_dim)
    joined = attended.reshape(seq_len, width).astype(jnp.bfloat16)
    after = resid + jnp.dot(joined, w_out, preferred_element_type=jnp.float32)
    normed_mid, normed_two, inverse_two = norm_parts(after, gain_two, shift_two)
    hidden_two = normed_mid.astype(jnp.bfloat16)
    pre = jnp.dot(hidden_two, w_up, preferred_element_type=jnp.float32)
    act_value, gelu_back = jax.vjp(lambda inner: jax.nn.gelu(inner, approximate=True), pre)
    act = act_value.astype(jnp.bfloat16)
    final = after + jnp.dot(act, w_down, preferred_element_type=jnp.float32)
    mixed = final.astype(jnp.bfloat16)[None]
    grad_final = cotangent[0].astype(jnp.float32)
    grad_mlp = cotangent[0]
    grad_w_down = jnp.dot(act.T, grad_mlp, preferred_element_type=jnp.float32)
    grad_act = jnp.dot(grad_mlp, w_down.T, preferred_element_type=jnp.float32)
    grad_pre = gelu_back(grad_act)[0].astype(jnp.bfloat16)
    grad_w_up = jnp.dot(hidden_two.T, grad_pre, preferred_element_type=jnp.float32)
    grad_hidden_two = jnp.dot(grad_pre, w_up.T, preferred_element_type=jnp.float32)
    grad_after_norm, grad_gain_two, grad_shift_two = norm_back(
        grad_hidden_two, normed_two, inverse_two, gain_two
    )
    grad_after = grad_final + grad_after_norm
    grad_branch = grad_after.astype(jnp.bfloat16)
    grad_w_out = jnp.dot(joined.T, grad_branch, preferred_element_type=jnp.float32)
    grad_heads = jnp.dot(grad_branch, w_out.T, preferred_element_type=jnp.float32).astype(
        jnp.bfloat16
    )
    grad_heads = grad_heads.reshape(seq_len, heads, head_dim)
    grad_blocks = grad_heads.reshape(blocks, span, heads, head_dim)
    grad_gate = (
        jnp.einsum("bthe,hbe->bth", grad_blocks, mem_value, preferred_element_type=jnp.float32)
        * flag
    )
    grad_mem_value = jnp.einsum("bth,bthe->hbe", gate, grad_blocks.astype(jnp.float32))
    grad_score = grad_gate * sigma * (1.0 - sigma) * scale
    grad_query_mem = grad_score[..., None] * jnp.transpose(mem_key, (1, 0, 2))[:, None].astype(
        jnp.float32
    )
    grad_mem_key = jnp.einsum("bth,bthe->hbe", grad_score, query_blocks.astype(jnp.float32))
    grad_mem_kv = jnp.stack([grad_mem_key, grad_mem_value]).astype(jnp.bfloat16)
    grad_w_kv = jnp.einsum(
        "hbd,chbe->dche", memory, grad_mem_kv, preferred_element_type=jnp.float32
    ).reshape(width, 2 * width)
    grad_memory = jnp.einsum(
        "chbe,dche->hbd", grad_mem_kv, w_kv, preferred_element_type=jnp.float32
    ).astype(jnp.bfloat16)
    grad_memory_all = lax.all_gather(grad_memory[None], "basis", axis=0, tiled=True)
    grad_coeffs = jnp.einsum(
        "shbj,shbd->sjd", weights_e, grad_memory_all, preferred_element_type=jnp.float32
    )
    grad_query = grad_query_mem.reshape(seq_len, heads, head_dim)
    grad_key = jnp.zeros((seq_len, heads, head_dim), jnp.float32)
    grad_value = jnp.zeros((seq_len, heads, head_dim), jnp.float32)
    for index, first in enumerate(starts):
        finish = min(first + step, seq_len)
        scores = causal_scores(query[first:finish], key[:finish], first, scale)
        probs_full = jnp.exp(scores - log_totals[index])
        probs = probs_full.astype(jnp.bfloat16)
        upstream = grad_heads[first:finish]
        grad_probs = jnp.einsum(
            "qhe,khe->hqk", upstream, value[:finish], preferred_element_type=jnp.float32
        )
        grad_scores = probs_full * (
            grad_probs - jnp.sum(probs_full * grad_probs, axis=-1, keepdims=True)
        )
        grad_scores = grad_scores.astype(jnp.bfloat16)
        grad_value = grad_value.at[:finish].add(
            jnp.einsum("hqk,qhe->khe", probs, upstream, preferred_element_type=jnp.float32)
        )
        grad_key = grad_key.at[:finish].add(
            jnp.einsum(
                "hqk,qhe->khe", grad_scores, query[first:finish], preferred_element_type=jnp.float32
            )
            * scale
        )
        grad_query = grad_query.at[first:finish].add(
            jnp.einsum(
                "hqk,khe->qhe", grad_scores, key[:finish], preferred_element_type=jnp.float32
            )
            * scale
        )
    grad_qkv = (
        jnp.stack([grad_query, grad_key, grad_value], axis=1)
        .reshape(seq_len, 3 * width)
        .astype(jnp.bfloat16)
    )
    grad_w_qkv = jnp.dot(hidden_one.T, grad_qkv, preferred_element_type=jnp.float32)
    grad_w_qkv = grad_w_qkv.at[:, width:].add(grad_w_kv)
    grad_hidden_one = jnp.dot(grad_qkv, w_qkv.T, preferred_element_type=jnp.float32)
    grad_resid_norm, grad_gain_one, grad_shift_one = norm_back(
        grad_hidden_one, normed_one, inverse_one, gain_one
    )
    grad_tokens = (grad_after + grad_resid_norm)[None]
    grads_of = ((grad_w_down, 1), (grad_w_up, 2), (grad_w_out, 2), (grad_w_qkv, 2))
    small = jnp.stack([grad_gain_one, grad_shift_one, grad_gain_two, grad_shift_two])
    small = jnp.concatenate([small, jnp.zeros_like(small)], axis=0)
    folded = [fold(grad.astype(bf16), pieces) for grad, pieces in grads_of]
    arrays, widths_of = [], []
    for array in folded:
        third = array.shape[2] // 3
        arrays += [array[:, :, i * third : (i + 1) * third] for i in range(3)]
    *blocks_of, small = summed_shares(place, arrays, small)
    shares = []
    for i, (grad, pieces) in enumerate(grads_of):
        block = jnp.concatenate(blocks_of[3 * i : 3 * i + 3], axis=1)
        shares.append(halve_rest(place, unfold(block, pieces)))
    share_down, share_up, share_out, share_qkv = shares
    small = sum_rest(place, small)
    flat = lax.axis_index("dp") * place.basis + lax.axis_index("basis")
    part = width // (place.dp * place.basis)
    share_small = lax.dynamic_slice_in_dim(small, flat * part, part, 1)
    return (
        mixed,
        grad_tokens,
        grad_coeffs,
        share_qkv,
        share_out,
        share_up,
        share_down,
        share_small[0],
        share_small[1],
        share_small[2],
        share_small[3],
    )


def solution(mesh):
    in_specs = (
        P(("dp", "basis"), None, None),
        P(),
        P(),
        P(),
        P(),
        P(),
        P(),
        P(),
        P(),
        P("dp", "basis", None),
        P(("dp", "basis")),
        P("dp", None, None),
        P("dp", None, None),
        P(("dp", "basis"), None, None),
    )
    out_specs = (
        P(("dp", "basis"), None, None),
        P(("dp", "basis"), None, None),
        P("dp", "basis", None),
        P(("dp", "basis"), None),
        P(("dp", "basis"), None),
        P(("dp", "basis"), None),
        P(("dp", "basis"), None),
        P(("dp", "basis")),
        P(("dp", "basis")),
        P(("dp", "basis")),
        P(("dp", "basis")),
    )
    return jax.shard_map(
        functools.partial(on_device, Place(mesh.shape)), mesh=mesh, in_specs=in_specs, out_specs=out_specs, check_vma=False
    )
```

```python
import functools, math
import jax, jax.numpy as jnp
from jax import lax
from jax.experimental import pallas as pl
from jax.experimental.pallas import tpu as pltpu
from jax.sharding import PartitionSpec as P
f32 = jnp.float32; bf16 = jnp.bfloat16
eps = 1e-05
ANY = pl.BlockSpec(memory_space=pl.ANY)
VM = pl.BlockSpec(memory_space=pltpu.VMEM)
SM = pl.BlockSpec(memory_space=pltpu.SMEM)
LANES=128

def nn(a, b):
    return jnp.dot(a, b, preferred_element_type=f32)
def nt(a, b):
    return lax.dot_general(a, b, (((1,), (1,)), ((), ())), preferred_element_type=f32)
def tn(a, b):
    return lax.dot_general(a, b, (((0,), (0,)), ((), ())), preferred_element_type=f32)

def lanes_of(c):
    return pl.ds(pl.multiple_of(c * LANES, LANES), LANES)
def rows_of(i, n):
    return pl.ds(pl.multiple_of(i * n, n), n)

def query_blocks(seq):
    wide = 256
    return [(q, min(wide, seq - q)) for q in range(0, seq, wide)]

def causal(scores, first):
    keys, queries = scores.shape
    top, low = scores[:first], scores[first:]
    key = lax.broadcasted_iota(jnp.int32, low.shape, 0)
    query = lax.broadcasted_iota(jnp.int32, low.shape, 1)
    low = jnp.where(key <= query, low, -1e30)
    return low if first == 0 else jnp.concatenate([top, low], axis=0)

def norm_into(src, out, gain, shift, seq):
    def body(c, carry):
        at = lanes_of(c)
        x = src[:, at]
        cen = x - jnp.mean(x, axis=0, keepdims=True)
        inv = lax.rsqrt(jnp.mean(cen * cen, axis=0, keepdims=True) + eps)
        out[:, at] = (cen * inv * gain + shift).astype(out.dtype)
        return carry
    lax.fori_loop(0, seq // LANES, body, 0)

def mem_columns(block, head):
    lane = lax.broadcasted_iota(jnp.int32, block.shape, 1)
    wide = block.astype(f32)
    return [jnp.sum(jnp.where(lane == 2 * head + b, wide, 0.0), axis=1, keepdims=True) for b in (0, 1)]

def by_block(columns, shape, span):
    lane = lax.broadcasted_iota(jnp.int32, shape, 1)
    return jnp.where(lane < span, columns[0], columns[1])

def forward_kernel(heads, span, scale,
    flag, tokens_h, norms, memory, w_qkv_h, w_out_h, w_up_h,
    h1_o, qkv_o, aux_o, joined_o, after_o, h2_o, act_o, slope_o,
    tokens, w_qkv, w_out, w_up, x, h1, qkv, aux, joined, after, h2, act, slope, in_sem, out_sem):
    seq, width = tokens.shape
    ff = w_up.shape[1]
    hd = width // heads
    loads = [pltpu.make_async_copy(s, d, in_sem.at[i]) for i, (s, d) in enumerate(
        [(tokens_h, tokens), (w_qkv_h, w_qkv), (w_out_h, w_out), (w_up_h, w_up)])]
    for l in loads: l.start()
    def put(i, src, dst):
        cp = pltpu.make_async_copy(src, dst, out_sem.at[i]); cp.start(); return cp
    puts = []
    gain = norms[:, 0:1]; shift = norms[:, 1:2]
    h1[:, seq:] = jnp.transpose(memory[...].astype(f32)).astype(bf16)
    loads[0].wait()
    def turn(c, carry):
        at = lanes_of(c)
        x[:, at] = jnp.transpose(tokens[at, :].astype(f32))
        return carry
    lax.fori_loop(0, seq // LANES, turn, 0)
    norm_into(x, h1, gain, shift, seq)
    puts.append(put(0, h1, h1_o))
    loads[1].wait()
    def project(i, carry):
        at = rows_of(i, width)
        qkv[at, :] = tn(w_qkv[:, at], h1[...]).astype(bf16)
        return carry
    lax.fori_loop(0, 3, project, 0)
    puts.append(put(1, qkv, qkv_o))
    on = flag[0].astype(f32)
    sub = lax.broadcasted_iota(jnp.int32, (8, seq), 0)

    def head_step(h, carry):
        base = pl.multiple_of(h * hd, hd)
        q = qkv[pl.ds(base, hd), :seq] * jnp.asarray(scale, bf16)
        kx = jnp.transpose(qkv[pl.ds(width + base, hd), :])
        v = qkv[pl.ds(2 * width + base, hd), :seq]
        outs, logs = [], []
        for first, n in query_blocks(seq):
            keys = first + n
            s = causal(nn(kx[:keys], q[:, first:keys]), first)
            peak = jnp.max(s, axis=0, keepdims=True)
            e = jnp.exp(s - peak)
            total = jnp.sum(e, axis=0, keepdims=True)
            outs.append(nn(v[:, :keys], e.astype(bf16)) / total)
            logs.append(peak + jnp.log(total))
        o = jnp.concatenate(outs, axis=1)
        log_total = jnp.concatenate(logs, axis=1)
        ms = nn(kx[seq:seq + 32], q)
        row = lax.broadcasted_iota(jnp.int32, ms.shape, 0)
        lane = lax.broadcasted_iota(jnp.int32, ms.shape, 1)
        want = 2 * h + jnp.where(lane < span, 0, 1)
        ms = jnp.sum(jnp.where(row == want, ms, 0.0), axis=0, keepdims=True)
        sig = jax.nn.sigmoid(ms)
        mv = by_block(mem_columns(qkv[pl.ds(2 * width + base, hd), seq:], h), (hd, seq), span)
        joined[pl.ds(base, hd), :] = (o + (sig * on) * mv).astype(bf16)
        aux[h] = jnp.where(sub == 0, log_total, jnp.where(sub == 1, sig, 0.0))
        return carry
    lax.fori_loop(0, heads, head_step, 0)
    puts.append(put(2, aux, aux_o))
    puts.append(put(3, joined, joined_o))
    loads[2].wait()
    after[...] = x[...] + tn(w_out[...], joined[...])
    puts.append(put(4, after, after_o))
    norm_into(after, h2, norms[:, 2:3], norms[:, 3:4], seq)
    puts.append(put(5, h2, h2_o))
    loads[3].wait()
    step = 512
    def up(i, carry):
        at = rows_of(i, step)
        pre = tn(w_up[:, at], h2[...])
        sq = pre * pre
        c = math.sqrt(2.0 / math.pi)
        t = jnp.tanh(pre * (c + (c * 0.044715) * sq))
        half = 0.5 + 0.5 * t
        act[at, :] = (pre * half).astype(bf16)
        slope[at, :] = (half + (0.5 * pre) * (1.0 - t * t) * (c + (3 * c * 0.044715) * sq)).astype(bf16)
        return carry
    lax.fori_loop(0, ff // step, up, 0)
    puts.append(put(6, act, act_o))
    puts.append(put(7, slope, slope_o))
    for p in puts: p.wait()

def forward(heads, blocks, flag, tokens, norms, memory, w_qkv, w_out, w_up):
    seq, width = tokens.shape
    ff = w_up.shape[1]
    wide = seq + LANES
    span = seq // blocks
    scale = 1.0 / math.sqrt(width // heads)
    S = jax.ShapeDtypeStruct
    outs = [((width, wide), bf16), ((3 * width, wide), bf16), ((heads, 8, seq), f32), ((width, seq), bf16),
            ((width, seq), f32), ((width, seq), bf16), ((ff, seq), bf16), ((ff, seq), bf16)]
    return pl.pallas_call(
        functools.partial(forward_kernel, heads, span, scale),
        out_shape=[S(*o) for o in outs],
        in_specs=[SM, ANY, VM, VM, ANY, ANY, ANY],
        out_specs=[ANY] * len(outs),
        scratch_shapes=[pltpu.VMEM(tokens.shape, bf16), pltpu.VMEM(w_qkv.shape, bf16), pltpu.VMEM(w_out.shape, bf16), pltpu.VMEM(w_up.shape, bf16),
            pltpu.VMEM((width, seq), f32)] + [pltpu.VMEM(*o) for o in outs] + [pltpu.SemaphoreType.DMA((4,)), pltpu.SemaphoreType.DMA((len(outs),))],
        compiler_params=pltpu.CompilerParams(vmem_limit_bytes=56 * 2**20),
    )(flag, tokens, norms, memory, w_qkv, w_out, w_up)

GROUP = 32
STAGES = 5
MESH = pl.DeviceIdType.MESH

class Place:
    def __init__(self, mesh_shape):
        self.dp, self.basis = mesh_shape["dp"], mesh_shape["basis"]
        self.bits = (self.dp * self.basis).bit_length() - 1
        self.low = self.bits - STAGES
        self.basis_bits = self.basis.bit_length() - 1

    def here(self):
        self.me_dp, self.me_basis = lax.axis_index("dp"), lax.axis_index("basis")
        flat = self.me_dp * self.basis + self.me_basis
        self.mine = [lax.rem(flat // (1 << (self.low + b)), 2) for b in range(STAGES)]

    def partner(self, b):
        flip = 1 - 2 * self.mine[b]
        bit = self.low + b
        if bit < self.basis_bits:
            return (self.me_dp, self.me_basis + flip * (1 << bit))
        return (self.me_dp + flip * (1 << (bit - self.basis_bits)), self.me_basis)

    def beside(self):
        return (self.me_dp, 1 - self.me_basis)

    def spot(self, block, order):
        where = 0
        for stage, b in enumerate(order):
            differs = 1 - self.mine[b] if (block >> b) & 1 else self.mine[b]
            where = where + differs * (1 << (STAGES - 1 - stage))
        return where


class Share:
    def __init__(self, place, order, own, recv, send_sem, recv_sem, columns=None):
        self.place, self.order, self.own, self.recv = place, order, own, recv
        self.send_sem, self.recv_sem = send_sem, recv_sem
        self.columns = own.shape[2] if columns is None else columns
        self.sent = None
        self.stage = 0

    def store(self, block, value, first=0):
        self.own[self.place.spot(block, self.order), :, first : first + value.shape[1]] = value.astype(bf16)

    def send(self):
        stage = self.stage
        count = GROUP >> (stage + 1)
        self.sent = pltpu.make_async_remote_copy(
            src_ref=self.own.at[pl.ds(count, count), :, pl.ds(0, self.columns)],
            dst_ref=self.recv.at[pl.ds(GROUP - 2 * count, count), :, pl.ds(0, self.columns)],
            send_sem=self.send_sem.at[stage],
            recv_sem=self.recv_sem.at[stage],
            device_id=self.place.partner(self.order[stage]),
            device_id_type=MESH,
        )
        self.sent.start()

    def pump(self):
        self.sent.wait()
        count = GROUP >> (self.stage + 1)
        self.stage += 1
        if self.stage == STAGES:
            return
        first = GROUP - 2 * count
        at = pl.ds(0, self.columns)

        def add(k, carry):
            self.own[k, :, at] = self.own[k, :, at] + self.recv[first + k, :, at]
            return carry

        lax.fori_loop(0, count, add, 0)
        self.send()

    def last(self):
        at = pl.ds(0, self.columns)
        return self.own[0, :, at].astype(f32) + self.recv[GROUP - 2, :, at].astype(f32)


class Whole:
    def __init__(self, place, own, recv, send_sem, recv_sem):
        self.place, self.own, self.recv = place, own, recv
        self.send_sem, self.recv_sem = send_sem, recv_sem
        self.stage = 0

    def send(self):
        stage = self.stage
        self.sent = pltpu.make_async_remote_copy(
            src_ref=self.own.at[stage], dst_ref=self.recv.at[stage],
            send_sem=self.send_sem.at[stage], recv_sem=self.recv_sem.at[stage],
            device_id=self.place.partner(stage), device_id_type=MESH)
        self.sent.start()

    def pump(self):
        self.sent.wait()
        stage = self.stage
        self.own[stage + 1] = self.own[stage] + self.recv[stage]
        self.stage += 1
        if self.stage < STAGES:
            self.send()


def greet(place):
    barrier = pltpu.get_barrier_semaphore()
    for b in range(STAGES):
        pl.semaphore_signal(barrier, inc=1, device_id=place.partner(b), device_id_type=MESH)
    if place.low > 0:
        pl.semaphore_signal(barrier, inc=1, device_id=place.beside(), device_id_type=MESH)
    pl.semaphore_wait(barrier, STAGES + (1 if place.low > 0 else 0))


ORDERS = ((1, 0, 2, 3, 4), (1, 2, 3, 0, 4), (1, 3, 0, 2, 4))


def norm_back(x_of, u_of, out, gain, acc_gain, acc_shift, chunks, base_of):
    acc_gain[...] = jnp.zeros_like(acc_gain)
    acc_shift[...] = jnp.zeros_like(acc_shift)

    def body(c, carry):
        at = lanes_of(c)
        x = x_of(c)
        cen = x - jnp.mean(x, axis=0, keepdims=True)
        inv = lax.rsqrt(jnp.mean(cen * cen, axis=0, keepdims=True) + eps)
        n = cen * inv
        u = u_of(c)
        un = u * n
        acc_gain[...] += un
        acc_shift[...] += u
        g = u * gain
        m1 = jnp.mean(g, axis=0, keepdims=True)
        m2 = jnp.mean(un * gain, axis=0, keepdims=True)
        out(c, base_of(c) + inv * (g - m1 - n * m2))
        return carry

    lax.fori_loop(0, chunks, body, 0)


def columns_sum(acc):
    return jnp.sum(jnp.transpose(acc[...]), axis=0, keepdims=True)


def backward_kernel(place, heads, span, scale,
    flag, norms, weights_e, dy_h, tokens_h, act_h, slope_h, h2_h, after_h, joined_h, qkv_h, aux_h, h1_h, w_down_h, w_up_h, w_out_h, w_qkv_h,
    mixed_o, gtok_o, gcoef_o, s_qkv, s_out, s_up, s_down, small_o,
    dy, act, slope, h2, joined, qkv, aux, h1, w_down, w_up, x, g, da, acc_a, acc_b, rows_small,
    own_d, own_u, own_o, recv_d, recv_u, recv_o, mem_own, mem_recv,
    small_own, small_recv, load_sem, out_sem, send_sem, recv_sem, ready_sem, mem_sem):
    width, seq = h2.shape
    ff = act.shape[0]
    hd = width // heads
    chunks = seq // LANES
    place.here()
    barrier_parts = None
    loads = {}

    def load(name, src, dst):
        cp = pltpu.make_async_copy(src, dst, load_sem.at[len(loads)])
        cp.start()
        loads[name] = cp

    load("dy", dy_h, dy)
    load("act", act_h, act)
    load("w_down", w_down_h, w_down)
    load("slope", slope_h, slope)
    load("h2", h2_h, h2)
    load("w_up", w_up_h, w_up)
    load("after", after_h, x)
    load("joined", joined_h, joined)
    load("qkv", qkv_h, qkv)
    load("aux", aux_h, aux)
    load("h1", h1_h, h1)
    greet(place)
    down = [Share(place, ORDERS[p], own_d.at[p], recv_d.at[p], send_sem.at[p], recv_sem.at[p]) for p in range(3)]
    up = [Share(place, ORDERS[p], own_u.at[p], recv_u.at[p], send_sem.at[3 + p], recv_sem.at[3 + p]) for p in range(3)]
    out = Share(place, ORDERS[2], own_o, recv_o, send_sem.at[6], recv_sem.at[6])
    small = Whole(place, small_own, small_recv, send_sem.at[7], recv_sem.at[7])
    part_q = 3 * width // 6
    qs = [Share(place, ORDERS[p], own_d.at[p], recv_d.at[p], send_sem.at[8 + p], recv_sem.at[8 + p], columns=part_q) for p in range(3)]
    for p in range(3): qs[p].columns = part_q
    r_d = ff // GROUP
    r = width // GROUP
    half_d = r_d // 2

    loads["dy"].wait()
    loads["act"].wait()
    wide = width // 3
    for p in range(3):
        for piece in range(4):
            blocks = GROUP // 4
            val = nn(act[piece * blocks * r_d : (piece + 1) * blocks * r_d, :], dy[:, p * wide : (p + 1) * wide])
            for j in range(blocks):
                v = val[j * r_d : (j + 1) * r_d]
                down[p].store(piece * blocks + j, jnp.concatenate([v[:half_d], v[half_d:]], axis=1))
        down[p].send()
    loads["w_down"].wait()
    loads["slope"].wait()
    step = 768

    def back_act(i, carry):
        at = rows_of(i, step)
        ga = nt(w_down[at, :], dy[...])
        slope[at, :] = (ga * slope[at, :].astype(f32)).astype(bf16)
        return carry

    down[0].pump()
    lax.fori_loop(0, 2, back_act, 0)
    down[1].pump()
    down[2].pump()
    lax.fori_loop(2, ff // step, back_act, 0)
    gp = slope
    loads["h2"].wait()
    half_up = ff // 2
    fold = half_up // 3
    sub = 256
    for p in range(3):
        for q in range(fold // sub):
            at = p * fold + q * sub
            left = nt(h2[...], gp[at : at + sub, :])
            right = nt(h2[...], gp[half_up + at : half_up + at + sub, :])
            for j in range(GROUP):
                v = jnp.concatenate([left[j * r : (j + 1) * r], right[j * r : (j + 1) * r]], axis=0)
                up[p].store(j, v, q * sub)
        up[p].send()
        if p > 0:
            up[p - 1].pump()
    down[0].pump()
    loads["w_up"].wait()
    third = width // 3
    for i in range(3):
        g[i * third : (i + 1) * third, :] = nn(w_up[i * third : (i + 1) * third, :], gp[...])
        if i == 0:
            up[2].pump()
            down[1].pump()
            down[2].pump()
    load("w_qkv", w_qkv_h, w_up.at[:, pl.ds(0, 3 * width)])
    load("w_out", w_out_h, w_up.at[:, pl.ds(3 * width, width)])
    w_qkv = w_up.at[:, pl.ds(0, 3 * width)]
    w_out = w_up.at[:, pl.ds(3 * width, width)]
    loads["after"].wait()

    def keep_after(c, value):
        at = lanes_of(c)
        g[:, at] = value
        da[:, at] = value.astype(bf16)

    norm_back(lambda c: x[:, lanes_of(c)], lambda c: g[:, lanes_of(c)], keep_after, norms[:, 2:3], acc_a, acc_b, chunks,
              lambda c: jnp.transpose(dy[lanes_of(c), :].astype(f32)))
    rows_small[2:3, :] = columns_sum(acc_a)
    rows_small[3:4, :] = columns_sum(acc_b)
    for d in down: d.pump()
    loads["joined"].wait()
    half_o = width // 2
    left = nt(joined[...], da[:half_o, :])
    right = nt(joined[...], da[half_o:, :])
    for j in range(GROUP):
        out.store(j, jnp.concatenate([left[j * r : (j + 1) * r], right[j * r : (j + 1) * r]], axis=0))
    out.send()
    loads["w_out"].wait()
    datt = h2
    datt[...] = nn(w_out[...], da[...]).astype(bf16)
    for d in down: d.pump()
    out.pump()
    loads["qkv"].wait()
    loads["aux"].wait()
    on = flag[0].astype(f32)

    def head_step(h, carry):
        base = pl.multiple_of(h * hd, hd)
        at_q, at_k, at_v = pl.ds(base, hd), pl.ds(width + base, hd), pl.ds(2 * width + base, hd)
        q = qkv[at_q, :seq] * jnp.asarray(scale, bf16)
        k = qkv[at_k, :seq]
        kt = jnp.transpose(k)
        vt = jnp.transpose(qkv[at_v, :seq])
        ks = k * jnp.asarray(scale, bf16)
        do = datt[at_q, :]
        log_total = aux[h, 0:1, :]
        dq, dk, dv = [], [], []
        for first, n in query_blocks(seq):
            keys = first + n
            qb, db = q[:, first:keys], do[:, first:keys]
            s = causal(nn(kt[:keys], qb), first)
            p = jnp.exp(s - log_total[:, first:keys])
            dp = nn(vt[:keys], db)
            ds = (p * (dp - jnp.sum(p * dp, axis=0, keepdims=True))).astype(bf16)
            dq.append(nn(ks[:, :keys], ds))
            dk.append(nt(qb, ds))
            dv.append(nt(db, p.astype(bf16)))
        def add_up(parts):
            total = parts[-1]
            for part in reversed(parts[:-1]):
                have = part.shape[1]
                total = jnp.concatenate([total[:, :have] + part, total[:, have:]], axis=1)
            return total
        dqt, dkt, dvt = jnp.concatenate(dq, axis=1), add_up(dk), add_up(dv)
        sig = aux[h, 1:2, :]
        mk = mem_columns(qkv[at_k, seq:], h)
        mv = mem_columns(qkv[at_v, seq:], h)
        dof = do.astype(f32)
        lane = lax.broadcasted_iota(jnp.int32, (1, seq), 1)
        dgate = on * jnp.sum(dof * by_block(mv, dof.shape, span), axis=0, keepdims=True)
        dscore = dgate * sig * (1.0 - sig) * scale
        dqt = dqt + dscore * by_block(mk, dof.shape, span)
        qf = qkv[at_q, :seq].astype(f32) * dscore
        vf = dof * (sig * on)
        mem_lane = lax.broadcasted_iota(jnp.int32, (hd, LANES), 1)
        def split(wide):
            total = jnp.sum(wide, axis=1, keepdims=True)
            low = jnp.sum(jnp.where(lane < span, wide, 0.0), axis=1, keepdims=True)
            return jnp.where(mem_lane == 2 * h, low, jnp.where(mem_lane == 2 * h + 1, total - low, 0.0)).astype(bf16)
        qkv[at_q, :seq] = dqt.astype(bf16)
        qkv[at_q, seq:] = jnp.zeros((hd, LANES), bf16)
        qkv[at_k, :seq] = dkt.astype(bf16)
        qkv[at_k, seq:] = split(qf)
        qkv[at_v, :seq] = dvt.astype(bf16)
        qkv[at_v, seq:] = split(vf)
        return carry

    quarter = heads // 4
    lax.fori_loop(0, quarter, head_step, 0)
    for d in down: d.pump()
    for u in up: u.pump()
    for p in range(3):
        v = down[p].last()
        s_down[:half_d, p * wide : (p + 1) * wide] = v[:, :wide]
        s_down[half_d:, p * wide : (p + 1) * wide] = v[:, wide:]
    for b in range(STAGES):
        pl.semaphore_signal(ready_sem.at[b], inc=1, device_id=place.partner(b), device_id_type=MESH)
    lax.fori_loop(quarter, 2 * quarter, head_step, 0)
    for u in up: u.pump()
    out.pump()
    lax.fori_loop(2 * quarter, 3 * quarter, head_step, 0)
    for u in up: u.pump()
    out.pump()
    lax.fori_loop(3 * quarter, heads, head_step, 0)
    for u in up: u.pump()
    out.pump()
    loads["h1"].wait()
    for b in range(STAGES):
        pl.semaphore_wait(ready_sem.at[b], 1)
    half_q = 3 * width // 2
    for p in range(3):
        at = p * part_q
        left = nt(h1[...], qkv[at : at + part_q, :])
        right = nt(h1[...], qkv[half_q + at : half_q + at + part_q, :])
        for j in range(GROUP):
            qs[p].store(j, jnp.concatenate([left[j * r : (j + 1) * r], right[j * r : (j + 1) * r]], axis=0))
        qs[p].send()
        if p > 0: qs[p - 1].pump()
    loads["w_qkv"].wait()
    gm = [None] * 3
    for i in range(3):
        val = nn(w_qkv[i * third : (i + 1) * third, :], qkv[...])
        x[i * third : (i + 1) * third, :] = val[:, :seq]
        gm[i] = val[:, seq:]
        if i == 0: qs[2].pump()
    mem_own[...] = jnp.transpose(jnp.concatenate(gm, axis=0))[:32].astype(bf16)
    mem_copy = pltpu.make_async_remote_copy(src_ref=mem_own, dst_ref=mem_recv, send_sem=mem_sem.at[0], recv_sem=mem_sem.at[1],
        device_id=place.beside(), device_id_type=MESH)
    mem_copy.start()
    load("tokens", tokens_h, dy)
    out.pump()
    for p in range(3):
        v = up[p].last()
        s_up[:, p * fold : (p + 1) * fold] = v[:r]
        s_up[:, half_up + p * fold : half_up + (p + 1) * fold] = v[r:]
    v = out.last()
    s_out[:, :half_o] = v[:r]
    s_out[:, half_o:] = v[r:]
    loads["tokens"].wait()

    def keep_tokens(c, value):
        gtok_o[lanes_of(c), :] = jnp.transpose(value)

    norm_back(lambda c: jnp.transpose(dy[lanes_of(c), :].astype(f32)), lambda c: x[:, lanes_of(c)], keep_tokens, norms[:, 0:1],
              acc_a, acc_b, chunks, lambda c: g[:, lanes_of(c)])
    rows_small[0:1, :] = columns_sum(acc_a)
    rows_small[1:2, :] = columns_sum(acc_b)
    rows_small[4:8, :] = jnp.zeros((4, width), f32)
    small_own[0] = rows_small[...]
    small.send()
    load("after2", after_h, x)
    for q in qs: q.pump()
    mem_copy.wait()
    me = place.me_basis
    gcoef_o[me] = tn(weights_e[me], mem_own[...])
    gcoef_o[1 - me] = tn(weights_e[1 - me], mem_recv[...])
    small.pump()
    loads["after2"].wait()
    for i in range(3):
        cols = slice(i * third, (i + 1) * third)
        val = tn(w_down[:, cols], act[...])
        mixed_o[:, cols] = jnp.transpose(x[cols, :] + val).astype(bf16)
        for q in qs:
            if q.stage < STAGES: q.pump()
        small.pump()
    for s in (small,):
        while s.stage < STAGES: s.pump()
    for p in range(3):
        while qs[p].stage < STAGES: qs[p].pump()
        v = qs[p].last()
        s_qkv[:, p * part_q : (p + 1) * part_q] = v[:r]
        s_qkv[:, half_q + p * part_q : half_q + (p + 1) * part_q] = v[r:]
    small_o[...] = small_own[STAGES]


def backward(place, heads, blocks, flag, norms, weights_e, dy, tokens, w_down, w_up, w_out, w_qkv, kept):
    h1, qkv, aux, joined, after, h2, act, slope = kept
    seq, width = dy.shape
    ff = w_up.shape[1]
    span = seq // blocks
    scale = 1.0 / math.sqrt(width // heads)
    r, r_d = width // GROUP, ff // GROUP
    S = jax.ShapeDtypeStruct
    outs = [((seq, width), bf16), ((seq, width), f32), ((2, weights_e.shape[2], width), f32), ((r, 3 * width), f32), ((r, width), f32),
            ((r, ff), f32), ((r_d, width), f32), ((8, width), f32)]
    vm = lambda s, d: pltpu.VMEM(s, d)
    part = ((r_d // 2), 2 * width // 3)
    part_o = (2 * r, width // 2)
    scratch = [vm((seq, width), bf16), vm((ff, seq), bf16), vm((ff, seq), bf16), vm((width, seq), bf16), vm((width, seq), bf16),
        vm(qkv.shape, bf16), vm(aux.shape, f32), vm(h1.shape, bf16), vm(w_down.shape, bf16), vm(w_up.shape, bf16),
        vm((width, seq), f32), vm((width, seq), f32), vm((width, seq), bf16), vm((width, LANES), f32), vm((width, LANES), f32), vm((8, width), f32),
        vm((3, GROUP) + part, bf16), vm((3, GROUP) + part, bf16), vm((GROUP,) + part_o, bf16),
        vm((3, GROUP - 1) + part, bf16), vm((3, GROUP - 1) + part, bf16), vm((GROUP - 1,) + part_o, bf16),
        vm((32, width), bf16), vm((32, width), bf16), vm((STAGES + 1, 8, width), f32), vm((STAGES, 8, width), f32),
        pltpu.SemaphoreType.DMA((15,)), pltpu.SemaphoreType.DMA((4,)), pltpu.SemaphoreType.DMA((11, STAGES)), pltpu.SemaphoreType.DMA((11, STAGES)),
        pltpu.SemaphoreType.REGULAR((STAGES,)), pltpu.SemaphoreType.DMA((2,))]
    return pl.pallas_call(
        functools.partial(backward_kernel, place, heads, span, scale),
        out_shape=[S(*o) for o in outs],
        in_specs=[SM, VM, VM] + [ANY] * 14,
        out_specs=[VM] * len(outs),
        scratch_shapes=scratch,
        compiler_params=pltpu.CompilerParams(vmem_limit_bytes=60 * 2**20, collective_id=0, has_side_effects=True),
    )(flag, norms, weights_e, dy, tokens, act, slope, h2, after, joined, qkv, aux, h1, w_down, w_up, w_out, w_qkv)


def halve_rest(place, rows):
    for bit in reversed(range(place.low)):
        half = rows.shape[0] // 2
        if bit < place.basis_bits:
            axis, size, mask = "basis", place.basis, 1 << bit
        else:
            axis, size, mask = "dp", place.dp, 1 << (bit - place.basis_bits)
        mine = (lax.axis_index(axis) // mask) % 2
        keep = lax.dynamic_slice_in_dim(rows, mine * half, half, 0)
        give = lax.dynamic_slice_in_dim(rows, (1 - mine) * half, half, 0)
        rows = keep + lax.ppermute(give, axis, [(i, i ^ mask) for i in range(size)])
    return rows


def sum_rest(place, values):
    for bit in range(place.low):
        if bit < place.basis_bits:
            axis, size, mask = "basis", place.basis, 1 << bit
        else:
            axis, size, mask = "dp", place.dp, 1 << (bit - place.basis_bits)
        values = values + lax.ppermute(values, axis, [(i, i ^ mask) for i in range(size)])
    return values


def basis_weights(centres, widths, rows):
    spread = (widths * widths).astype(f32) + 4.0
    gap = centres[..., None].astype(f32) - rows.astype(f32)
    return 2.0 * lax.rsqrt(spread)[..., None] * jnp.exp(-gap * gap / (2.0 * spread[..., None]))


def on_device(place, tokens, w_qkv, w_out, w_up, w_down, gain_one, shift_one, gain_two, shift_two, coeffs, flags, centres, widths, cotangent):
    width = tokens.shape[2]
    local = coeffs.shape[1]
    heads, blocks = centres.shape[1], centres.shape[2]
    norms = jnp.stack([gain_one, shift_one, gain_two, shift_two], axis=1)
    rows = lax.axis_index("basis") * local + jnp.arange(local, dtype=jnp.int32)
    weights_e = basis_weights(centres, widths, rows).astype(bf16).reshape(2, heads * blocks, local)
    weights_e = jnp.pad(weights_e, ((0, 0), (0, 32 - heads * blocks), (0, 0)))
    partial_mem = jnp.einsum("srj,sjd->srd", weights_e, coeffs, preferred_element_type=f32)
    me = lax.axis_index("basis")
    give = lax.dynamic_index_in_dim(partial_mem, 1 - me, 0, keepdims=False).astype(bf16)
    keep = lax.dynamic_index_in_dim(partial_mem, me, 0, keepdims=False)
    got = lax.ppermute(give, "basis", [(0, 1), (1, 0)])
    memory = (keep + got.astype(f32)).astype(bf16)
    memory = jnp.pad(memory, ((0, LANES - 32), (0, 0)))
    kept = forward(heads, blocks, flags, tokens[0], norms, memory, w_qkv, w_out, w_up)
    mixed, gtok, gcoef, s_qkv, s_out, s_up, s_down, small = backward(
        place, heads, blocks, flags, norms, weights_e, cotangent[0], tokens[0], w_down, w_up, w_out, w_qkv, kept)
    small = sum_rest(place, small)
    flat = lax.axis_index("dp") * place.basis + lax.axis_index("basis")
    part = width // (place.dp * place.basis)
    small = lax.dynamic_slice_in_dim(small, flat * part, part, 1)
    return (mixed[None], gtok[None], gcoef, *(halve_rest(place, s) for s in (s_qkv, s_out, s_up, s_down)), small[0], small[1], small[2], small[3])


def solution(mesh):
    both = ("dp", "basis")
    in_specs = (P(both, None, None),) + (P(),) * 8 + (P("dp", "basis", None), P(both), P("dp", None, None), P("dp", None, None), P(both, None, None))
    out_specs = (P(both, None, None), P(both, None, None), P("dp", "basis", None)) + (P(both, None),) * 4 + (P(both),) * 4
    return jax.shard_map(functools.partial(on_device, Place(mesh.shape)), mesh=mesh, in_specs=in_specs, out_specs=out_specs, check_vma=False)
```

```python
import functools
import math

import jax
import jax.numpy as jnp
from jax import lax
from jax.experimental import pallas as pl
from jax.experimental.pallas import tpu as pltpu
from jax.sharding import PartitionSpec as P

f32 = jnp.float32
bf16 = jnp.bfloat16
eps = 1e-05
ANY = pl.BlockSpec(memory_space=pl.ANY)
VM = pl.BlockSpec(memory_space=pltpu.VMEM)
SM = pl.BlockSpec(memory_space=pltpu.SMEM)
MESH = pl.DeviceIdType.MESH
LANES = 128
MEM = 32
GROUP = 32
STAGES = 5
FORWARD_HEADS = 4


def nn(a, b):
    return jnp.dot(a, b, preferred_element_type=f32)


def nt(a, b):
    return lax.dot_general(a, b, (((1,), (1,)), ((), ())), preferred_element_type=f32)


def tn(a, b):
    return lax.dot_general(a, b, (((0,), (0,)), ((), ())), preferred_element_type=f32)


def lanes_of(c):
    return pl.ds(pl.multiple_of(c * LANES, LANES), LANES)


def rows_of(i, n):
    return pl.ds(pl.multiple_of(i * n, n), n)


def query_blocks(seq):
    wide = 256
    return [(q, min(wide, seq - q)) for q in range(0, seq, wide)]


def causal(scores, first):
    top, low = scores[:first], scores[first:]
    key = lax.broadcasted_iota(jnp.int32, low.shape, 0)
    query = lax.broadcasted_iota(jnp.int32, low.shape, 1)
    low = jnp.where(key <= query, low, -1e30)
    return low if first == 0 else jnp.concatenate([top, low], axis=0)


def norm_stats(x):
    cen = x - jnp.mean(x, axis=0, keepdims=True)
    inv = lax.rsqrt(jnp.mean(cen * cen, axis=0, keepdims=True) + eps)
    return cen * inv, inv


def own_head(shape, samples, features, head_dim):
    sample = lax.broadcasted_iota(jnp.int32, shape, samples)
    first = lax.rem(sample, 16) * head_dim
    feature = lax.broadcasted_iota(jnp.int32, shape, features)
    return (sample < MEM) & (feature >= first) & (feature < first + head_dim)


def two_parts(values):
    high = values.astype(bf16)
    low = (values - high.astype(f32)).astype(bf16)
    return jnp.concatenate([high, low, jnp.zeros((LANES - 2 * MEM, values.shape[1]), bf16)], axis=0)


def add_up(parts):
    total = parts[-1]
    for part in reversed(parts[:-1]):
        have = part.shape[1]
        total = jnp.concatenate([total[:, :have] + part, total[:, have:]], axis=1)
    return total


def ahead(count, product, use):
    have = product(0)
    for i in range(count):
        following = product(i + 1) if i + 1 < count else None
        use(i, have)
        have = following


def columns_sum(acc):
    return jnp.sum(jnp.transpose(acc[...]), axis=0, keepdims=True)


class Place:
    def __init__(self, mesh_shape):
        self.dp, self.basis = mesh_shape["dp"], mesh_shape["basis"]
        self.bits = (self.dp * self.basis).bit_length() - 1
        self.low = self.bits - STAGES
        self.basis_bits = self.basis.bit_length() - 1

    def here(self):
        self.me_dp, self.me_basis = lax.axis_index("dp"), lax.axis_index("basis")
        flat = self.me_dp * self.basis + self.me_basis
        self.mine = [lax.rem(flat // (1 << (self.low + b)), 2) for b in range(STAGES)]

    def partner(self, bits):
        to_dp, to_basis = self.me_dp, self.me_basis
        for b in bits:
            flip = 1 - 2 * self.mine[b]
            bit = self.low + b
            if bit < self.basis_bits:
                to_basis = to_basis + flip * (1 << bit)
            else:
                to_dp = to_dp + flip * (1 << (bit - self.basis_bits))
        return (to_dp, to_basis)

    def beside(self):
        return (self.me_dp, 1 - self.me_basis)

    def spot(self, block, order):
        where = 0
        for b in (b for bits in order for b in bits):
            where = 2 * where + (1 - self.mine[b] if (block >> b) & 1 else self.mine[b])
        return where

    def greet(self):
        barrier = pltpu.get_barrier_semaphore()
        for bits in PARTNERS:
            pl.semaphore_signal(barrier, inc=1, device_id=self.partner(bits), device_id_type=MESH)
        if self.low > 0:
            pl.semaphore_signal(barrier, inc=1, device_id=self.beside(), device_id_type=MESH)

    def greeted(self):
        pl.semaphore_wait(pltpu.get_barrier_semaphore(), len(PARTNERS) + (1 if self.low > 0 else 0))


PARTNERS = ((0,), (1,), (2,), (3,), (4,), (0, 2), (3, 4))
ORDERS = (((1,), (0,), (2,), (3,), (4,)), ((1,), (2,), (3,), (0,), (4,)), ((1,), (3,), (0,), (2,), (4,)))
LATE_ORDERS = (((1,), (0,), (2,), (3, 4)), ((1,), (2,), (0,), (3, 4)), ((1,), (0, 2), (3, 4)))
SMALL_ORDER = ((1,), (0, 2), (3, 4))


def flips(bits):
    return [bits] if len(bits) == 1 else [bits[1:], bits[:1], bits]


class Share:
    def __init__(self, place, order, own, recv, rows, columns, send_sem, recv_sem, ready_sem=None, before=None):
        self.place, self.order = place, order
        (self.own, row, column), (self.recv, recv_row, recv_column) = own, recv
        self.row, self.column = row, column
        self.at = (pl.ds(row, rows), pl.ds(column, columns))
        self.recv_at = (pl.ds(recv_row, rows), pl.ds(recv_column, columns))
        self.send_sem, self.recv_sem = send_sem, recv_sem
        self.ready_sem, self.before = ready_sem, before
        self.stage, self.sent, self.left = 0, 0, GROUP
        self.all_copies = []

    def store(self, block, value, first=0):
        rows, columns = value.shape
        at = (pl.ds(self.row, rows), pl.ds(self.column + first, columns))
        self.own[(self.place.spot(block, self.order), *at)] = value.astype(bf16)

    def send(self):
        self.part = self.left >> len(self.order[self.stage])
        self.copies = []
        for i, bits in enumerate(flips(self.order[self.stage])):
            if self.before is not None:
                pl.semaphore_wait(self.before.ready_sem.at[self.stage], 1)
            copy = pltpu.make_async_remote_copy(
                src_ref=self.own.at[(pl.ds((i + 1) * self.part, self.part), *self.at)],
                dst_ref=self.recv.at[(pl.ds(GROUP - self.left + i * self.part, self.part), *self.recv_at)],
                send_sem=self.send_sem.at[self.sent],
                recv_sem=self.recv_sem.at[self.sent],
                device_id=self.place.partner(bits),
                device_id_type=MESH,
            )
            copy.start()
            self.sent += 1
            self.copies.append(copy)
        self.all_copies += self.copies

    def tell(self, stage):
        if self.ready_sem is not None:
            to = self.place.partner(self.order[stage])
            pl.semaphore_signal(self.ready_sem.at[stage], inc=1, device_id=to, device_id_type=MESH)

    def pump(self):
        for copy in self.copies:
            copy.wait_recv()
        part, first, count = self.part, GROUP - self.left, len(self.copies)
        self.stage += 1
        if self.stage == len(self.order):
            for copy in self.all_copies:
                copy.wait_send()
            return

        def add(k, carry):
            here = (k, *self.at)
            total = self.own[here]
            for i in range(count):
                total = total + self.recv[(first + i * part + k, *self.recv_at)]
            self.own[here] = total
            return carry

        lax.fori_loop(0, part, add, 0, unroll=min(4, part))
        self.left = part
        self.tell(self.stage - 1)
        self.send()

    def done(self):
        return self.stage == len(self.order)

    def last(self):
        total = self.own[(0, *self.at)].astype(f32)
        for i in range(len(self.copies)):
            total = total + self.recv[(GROUP - self.left + i, *self.recv_at)].astype(f32)
        self.tell(len(self.order) - 1)
        return total


class Whole:
    def __init__(self, place, order, own, recv, send_sem, recv_sem):
        self.place, self.order, self.own, self.recv = place, order, own, recv
        self.send_sem, self.recv_sem = send_sem, recv_sem
        self.stage, self.sent = 0, 0

    def send(self):
        self.copies = []
        for bits in flips(self.order[self.stage]):
            copy = pltpu.make_async_remote_copy(
                src_ref=self.own.at[self.stage],
                dst_ref=self.recv.at[self.sent],
                send_sem=self.send_sem.at[self.sent],
                recv_sem=self.recv_sem.at[self.sent],
                device_id=self.place.partner(bits),
                device_id_type=MESH,
            )
            copy.start()
            self.sent += 1
            self.copies.append(copy)

    def pump(self):
        total = self.own[self.stage]
        for i, copy in enumerate(self.copies):
            copy.wait()
            total = total + self.recv[self.sent - len(self.copies) + i]
        self.stage += 1
        self.own[self.stage] = total
        if not self.done():
            self.send()

    def done(self):
        return self.stage == len(self.order)


VMEM_MIB = 63
PLAN = {
    "down0": (),
    "down1": (),
    "down2": (),
    "pre0": ("d0",),
    "pre1": ("d1",),
    "pre2": ("d2",),
    "pre3": (),
    "up0": (),
    "up1": (),
    "up2": (),
    "hid0": ("u0", "d0", "u1"),
    "hid1": ("u2", "d1"),
    "hid2": ("d2",),
    "norm2": ("d0",),
    "out": (),
    "att": (),
    "pair0": ("u2", "o", "u0"),
    "pair1": ("u1", "d1"),
    "pair2": ("d2", "d0"),
    "pair3": (),
    "a0": ("u2",),
    "a1": ("u0",),
    "a2": ("d1", "a0"),
    "pair4": ("d2", "d0", "o", "a1", "a2", "u2"),
    "pair5": ("u1",),
    "b0": ("d1",),
    "b1": (),
    "b2": (),
    "in0": ("a0", "u0", "b0", "d2", "b1", "b2", "u2", "a1"),
    "in1": ("o",),
    "in2": ("a2", "u1", "a0"),
    "sums": ("a1", "b0", "u0", "b1"),
    "back0": ("s", "a0", "b2"),
    "back1": ("a2", "u1", "o"),
    "coef": ("a1", "b0"),
    "mix0": ("b1", "s"),
    "mix1": ("a0", "a2", "b2"),
    "mix2": ("o",),
    "end": ("a1", "b0", "b1", "s", "a2"),
}


def layer_kernel(
    place,
    heads,
    span,
    scale,
    flag,
    centres,
    widths,
    gain_one,
    shift_one,
    gain_two,
    shift_two,
    tokens_h,
    coeffs_h,
    dy_h,
    w_qkv_h,
    w_out_h,
    w_up_h,
    w_down_h,
    mixed_o,
    gtok_o,
    gcoef_o,
    s_qkv_o,
    s_out_o,
    s_up_o,
    s_down_o,
    small_o,
    after_o,
    coeffs,
    dy,
    w_slot,
    w_down,
    x,
    g,
    h1,
    qkv,
    aux,
    joined,
    h2,
    act,
    slope,
    da,
    gcoef,
    acc_a,
    acc_b,
    norms,
    sig,
    k_dup,
    v_dup,
    v_rows,
    weights_e,
    mem_keep,
    s_qkv,
    s_out,
    s_up,
    s_down,
    own_d,
    recv_d,
    own_u0,
    own_u1,
    own_u2,
    recv_u0,
    recv_u1,
    recv_u2,
    own_o,
    recv_o,
    recv_b,
    mem_own,
    mem_recv,
    small_own,
    small_recv,
    load_sem,
    put_sem,
    send_sem,
    recv_sem,
    ready_sem,
    mem_sem,
):
    seq, width = dy.shape
    ff = act.shape[0]
    hd = width // heads
    chunks = seq // LANES
    r, r_d = width // GROUP, ff // GROUP
    third = width // 3
    place.here()
    me = place.me_basis
    loads, puts = {}, []

    def load(name, src, dst):
        loads[name] = pltpu.make_async_copy(src, dst, load_sem.at[len(loads)])
        loads[name].start()

    def put(src, dst):
        copy = pltpu.make_async_copy(src, dst, put_sem.at[len(puts)])
        copy.start()
        puts.append(copy)
        return copy

    slot_qkv, slot_out = w_slot.at[:, pl.ds(0, 3 * width)], w_slot.at[:, pl.ds(3 * width, width)]
    load("tokens", tokens_h, dy)
    load("coeffs", coeffs_h, coeffs)
    load("w_qkv", w_qkv_h, slot_qkv)
    place.greet()
    load("w_out", w_out_h, slot_out)
    load("w_down", w_down_h, w_down)

    given = [ref[...].reshape(1, width) for ref in (gain_one, shift_one, gain_two, shift_two)]
    norms[...] = jnp.transpose(jnp.concatenate(given + [jnp.zeros((LANES - 4, width), f32)], axis=0))

    local = coeffs.shape[1]
    place_of = me * local + lax.broadcasted_iota(jnp.int32, (MEM, local), 1)
    near = lax.broadcasted_iota(jnp.int32, (16, LANES), 0) == lax.broadcasted_iota(jnp.int32, (16, LANES), 1)

    def upright(ref, s):
        parts = []
        for b in range(2):
            row = jnp.concatenate([ref[s, b : b + 1, :], jnp.zeros((1, LANES - heads), jnp.int32)], axis=1).astype(f32)
            parts.append(jnp.sum(jnp.where(near, row, 0.0), axis=1, keepdims=True))
        return jnp.concatenate(parts, axis=0)

    row_id = lax.broadcasted_iota(jnp.int32, (MEM, local), 0)
    real = lax.rem(row_id, 16) < heads
    for s in range(2):
        c, w = upright(centres, s), upright(widths, s)
        spread = w * w + 4.0
        gap = c - place_of.astype(f32)
        value = 2.0 * lax.rsqrt(spread) * jnp.exp(-gap * gap / (2.0 * spread))
        weights_e[s] = jnp.where(real, value, 0.0).astype(bf16)
    loads["coeffs"].wait()
    mem_own[0] = nn(weights_e[1 - me], coeffs[1 - me]).astype(bf16)
    place.greeted()

    def to_beside(i):
        copy = pltpu.make_async_remote_copy(
            src_ref=mem_own.at[i],
            dst_ref=mem_recv.at[i],
            send_sem=mem_sem.at[i, 0],
            recv_sem=mem_sem.at[i, 1],
            device_id=place.beside(),
            device_id_type=MESH,
        )
        copy.start()
        return copy

    samples = to_beside(0)
    mem_keep[...] = nn(weights_e[me], coeffs[me])

    loads["tokens"].wait()

    def enter(c, carry):
        at = lanes_of(c)
        v = jnp.transpose(dy[at, :].astype(f32))
        x[:, at] = v
        n, _ = norm_stats(v)
        h1[:, at] = (n * norms[:, 0 : 1] + norms[:, 1 : 2]).astype(bf16)
        return carry

    lax.fori_loop(0, chunks, enter, 0)
    load("dy", dy_h, dy)
    loads["w_qkv"].wait()
    half_w = width // 2
    for i in range(2):
        at = i * half_w
        qkv[at : at + half_w, :seq] = tn(slot_qkv[:, at : at + half_w], h1[:, :seq]).astype(bf16)
    samples.wait()
    memory = (mem_keep[...] + mem_recv[0].astype(f32)).astype(bf16).astype(f32)
    memory = jnp.concatenate([memory, jnp.zeros((LANES - MEM, width), f32)], axis=0)
    h1[:, seq:] = jnp.transpose(memory).astype(bf16)

    def project(i):
        at = (i + 2) * half_w
        return tn(slot_qkv[:, at : at + half_w], h1[...])

    def keep_projected(i, value):
        at = (i + 2) * half_w
        qkv[at : at + half_w, :] = value.astype(bf16)

    ahead(4, project, keep_projected)
    load("w_up_a", w_up_h.at[:, pl.ds(0, 3 * width)], slot_qkv)
    on = flag[0].astype(f32)
    own_column = own_head((width, LANES), 1, 0, hd)
    mem_part = pl.ds(seq, LANES)
    in_block = lax.broadcasted_iota(jnp.int32, (MEM, seq), 0) // 16 == lax.broadcasted_iota(jnp.int32, (MEM, seq), 1) // span
    for i, dup, rows in ((1, k_dup, None), (2, v_dup, v_rows)):
        wide = jnp.where(own_column, qkv[i * width : (i + 1) * width, mem_part].astype(f32), 0.0)
        dup[...] = (wide + pltpu.roll(wide, MEM, 1)).astype(bf16)
        turned = jnp.transpose(wide)[:MEM]
        if rows is None:
            score = nn((turned * scale).astype(bf16), qkv[:width, :seq])
        else:
            rows[...] = turned.astype(bf16)
    sig[...] = jnp.where(in_block, jax.nn.sigmoid(score), 0.0)
    g[...] = nn(v_dup[...], two_parts(sig[...] * on))

    def heads_forward(i, carry):
        def scores(j):
            h = i * FORWARD_HEADS + j
            base = pl.multiple_of(h * hd, hd)
            q = qkv[pl.ds(base, hd), :seq] * jnp.asarray(scale, bf16)
            k = jnp.transpose(qkv[pl.ds(width + base, hd), :seq])
            return h, base, [nn(k[: first + n], q[:, first : first + n]) for first, n in query_blocks(seq)]

        def use(j, given):
            h, base, products = given
            weights, totals, logs = [], [], []
            for (first, n), s in zip(query_blocks(seq), products):
                s = causal(s, first)
                peak = jnp.max(s, axis=0, keepdims=True)
                e = jnp.exp(s - peak)
                weights.append(e.astype(bf16))
                totals.append(jnp.sum(e, axis=0, keepdims=True))
                logs.append(peak + jnp.log(totals[-1]))
            v = qkv[pl.ds(2 * width + base, hd), :seq]
            o = [nn(v[:, : e.shape[0]], e) / total for e, total in zip(weights, totals)]
            joined[pl.ds(base, hd), :] = (jnp.concatenate(o, axis=1) + g[pl.ds(base, hd), :]).astype(bf16)
            aux[h] = jnp.broadcast_to(jnp.concatenate(logs, axis=1), (8, seq))

        ahead(FORWARD_HEADS, scores, use)
        return carry

    lax.fori_loop(0, heads // FORWARD_HEADS, heads_forward, 0)
    loads["w_out"].wait()
    x[...] = x[...] + tn(slot_out[...], joined[...])
    load("w_up_b", w_up_h.at[:, pl.ds(3 * width, width)], slot_out)
    after_put = put(x, after_o)

    def second(c, carry):
        at = lanes_of(c)
        n, _ = norm_stats(x[:, at])
        h2[:, at] = (n * norms[:, 2 : 3] + norms[:, 3 : 4]).astype(bf16)
        return carry

    lax.fori_loop(0, chunks, second, 0)
    loads["w_up_a"].wait()
    step = 384

    def up_product(i):
        if i * step == 3 * width:
            loads["w_up_b"].wait()
        return tn(w_slot[:, i * step : (i + 1) * step], h2[...])

    def up_use(i, pre):
        sq = pre * pre
        c = math.sqrt(2.0 / math.pi)
        t = jnp.tanh(pre * (c + (c * 0.044715) * sq))
        half = 0.5 + 0.5 * t
        act[i * step : (i + 1) * step, :] = (pre * half).astype(bf16)
        rate = half + (0.5 * pre) * (1.0 - t * t) * (c + (3 * c * 0.044715) * sq)
        slope[i * step // r_d : (i + 1) * step // r_d] = rate.astype(bf16).reshape(step // r_d, r_d, seq)

    ahead(ff // step, up_product, up_use)

    half_d = r_d // 2
    all_shares = {}
    rows_o, columns_o = own_o.shape[1:]
    rows_d, columns_d = own_d.shape[2:]
    own_u, recv_u = (own_u0, own_u1, own_u2), (recv_u0, recv_u1, recv_u2)
    heads_a = heads * 2 // 3
    cols_a, cols_b = heads_a * hd, (heads - heads_a) * hd
    a, b = cols_a // 2, cols_b // 2

    def share(name, p, *where, orders=ORDERS, **more):
        i = len(all_shares)
        all_shares[name] = Share(place, orders[p], *where, send_sem.at[i], recv_sem.at[i], **more)

    for p in range(3):
        share(f"d{p}", p, (own_d.at[p], 0, 0), (recv_d.at[p], 0, 0), rows_d, columns_d, ready_sem=ready_sem.at[p])
    for p in range(3):
        share(f"u{p}", p, (own_u[p], 0, 0), (recv_u[p], 0, 0), *own_u[p].shape[1:])
    share("o", 2, (own_o, 0, 0), (recv_o, 0, 0), rows_o, columns_o)
    spots = {"a": ((0, 0), (0, a), (rows_o, 0)), "b": ((0, 2 * a), (rows_o, a), (rows_o, a + b))}
    for p in range(3):
        before = all_shares[f"d{p}"]
        share(f"a{p}", p, (slope, *spots["a"][p]), (recv_d.at[p], 0, 0), rows_o, a, before=before)
    for p in range(3):
        share(f"b{p}", p, (slope, *spots["b"][p]), (recv_b.at[p], 0, 0), rows_o, b, orders=LATE_ORDERS)
    small = Whole(place, SMALL_ORDER, small_own, small_recv, send_sem.at[13], recv_sem.at[13])
    all_shares["s"] = small

    def pump(names):
        for name in names:
            all_shares[name].pump()
            if name[0] == "d" and all_shares[name].done():
                v, p = all_shares[name].last(), int(name[1])
                s_down[:half_d, p * third : (p + 1) * third] = v[:, :third]
                s_down[half_d:, p * third : (p + 1) * third] = v[:, third:]

    loads["dy"].wait()
    blocks = GROUP // 4

    def down_product(i):
        p, piece = i // 4, i % 4
        return nn(act[piece * blocks * r_d : (piece + 1) * blocks * r_d, :], dy[:, p * third : (p + 1) * third])

    def down_use(i, val):
        p, piece = i // 4, i % 4
        for j in range(blocks):
            v = val[j * r_d : (j + 1) * r_d]
            all_shares[f"d{p}"].store(piece * blocks + j, jnp.concatenate([v[:half_d], v[half_d:]], axis=1))
        if piece == 3:
            all_shares[f"d{p}"].send()
            pump(PLAN[f"down{p}"])

    ahead(12, down_product, down_use)
    loads["w_down"].wait()

    def pre_product(i):
        return nt(w_down[i * step : (i + 1) * step, :], dy[...])

    def pre_use(i, val):
        at = slice(i * step // r_d, (i + 1) * step // r_d)
        rate = slope[at].reshape(step, seq).astype(f32)
        slope[at] = (val * rate).astype(bf16).reshape(step // r_d, r_d, seq)
        if i % 2 == 1:
            pump(PLAN[f"pre{i // 2}"])

    ahead(ff // step, pre_product, pre_use)
    half_up = ff // 2

    def slope_rows(first, count):
        low, high = first // r_d, -(-(first + count) // r_d)
        rows = slope[low:high].reshape((high - low) * r_d, seq)
        return rows[first - low * r_d : first - low * r_d + count]

    pieces, at = [], 0
    for p in range(3):
        part = own_u[p].shape[2]
        for sub in range(0, part, 256):
            count = min(256, part - sub)
            pieces.append((p, sub, at, count, sub + count == part))
            at += count

    def up_grad(i):
        _, _, at, count, _ = pieces[i]
        return nt(h2[...], slope_rows(at, count)), nt(h2[...], slope_rows(half_up + at, count))

    def up_grad_use(i, val):
        (p, sub, _, _, ends), (left, right) = pieces[i], val
        for j in range(GROUP):
            rows = slice(j * r, (j + 1) * r)
            all_shares[f"u{p}"].store(j, jnp.concatenate([left[rows], right[rows]], axis=0), sub)
        if ends:
            all_shares[f"u{p}"].send()
            pump(PLAN[f"up{p}"])

    ahead(len(pieces), up_grad, up_grad_use)
    for i in range(3):
        rows = slice(i * third, (i + 1) * third)
        g[rows, :] = nn(w_slot[rows, :], slope[...].reshape(ff, seq))
        pump(PLAN[f"hid{i}"])
    load("w_qkv2", w_qkv_h, slot_qkv)
    load("w_out2", w_out_h, slot_out)

    acc_b[...] = jnp.zeros_like(acc_b)
    acc_a[...] = jnp.zeros_like(acc_a)

    def second_back(c, carry):
        at = lanes_of(c)
        n, inv = norm_stats(x[:, at])
        u = g[:, at]
        un = u * n
        acc_b[...] += un
        acc_a[...] += u
        ug = u * norms[:, 2 : 3]
        m1 = jnp.mean(ug, axis=0, keepdims=True)
        m2 = jnp.mean(un * norms[:, 2 : 3], axis=0, keepdims=True)
        v = jnp.transpose(dy[at, :].astype(f32)) + inv * (ug - m1 - n * m2)
        g[:, at] = v
        da[:, at] = v.astype(bf16)
        return carry

    lax.fori_loop(0, chunks, second_back, 0)
    load("tokens2", tokens_h, dy)
    small_own[0, 2:3, :] = columns_sum(acc_b)
    small_own[0, 3:4, :] = columns_sum(acc_a)
    small_own[0, 4:8, :] = jnp.zeros((4, width), f32)
    pump(PLAN["norm2"])
    half_o = width // 2
    left, right = nt(joined[...], da[:half_o, :]), nt(joined[...], da[half_o:, :])
    for j in range(GROUP):
        rows = slice(j * r, (j + 1) * r)
        all_shares["o"].store(j, jnp.concatenate([left[rows], right[rows]], axis=0))
    all_shares["o"].send()
    pump(PLAN["out"])
    loads["w_out2"].wait()
    datt = h2
    datt[...] = nn(slot_out[...], da[...]).astype(bf16)
    pump(PLAN["att"])

    gates = sig[...]
    dscore = two_parts((on * scale) * nn(v_rows[...], datt[...]) * gates * (1.0 - gates))
    after_put.wait()
    x[...] = nn(k_dup[...], dscore)
    for i, wide in ((1, nt(qkv[:width, :seq], dscore)), (2, nt(datt[...], two_parts(gates * on)))):
        total = wide + pltpu.roll(wide, LANES - MEM, 1)
        qkv[i * width : (i + 1) * width, mem_part] = jnp.where(own_column, total, 0.0).astype(bf16)
    qkv[:width, mem_part] = jnp.zeros((width, LANES), bf16)

    def pair_back(i):
        todo = []
        for h in (2 * i, 2 * i + 1):
            at_q, at_k, at_v = (slice(j * width + h * hd, j * width + (h + 1) * hd) for j in range(3))
            q = qkv[at_q, :seq] * jnp.asarray(scale, bf16)
            k = qkv[at_k, :seq]
            k_up, v_up = jnp.transpose(k), jnp.transpose(qkv[at_v, :seq])
            do = datt[at_q, :]
            s = [nn(k_up[: first + n], q[:, first : first + n]) for first, n in query_blocks(seq)]
            dp = [nn(v_up[: first + n], do[:, first : first + n]) for first, n in query_blocks(seq)]
            todo.append((h, at_q, at_k, at_v, q, k * jnp.asarray(scale, bf16), do, s, dp))
        ready = []
        for h, at_q, at_k, at_v, q, k, do, scores, grads in todo:
            log_total = aux[h, 0:1, :]
            ps, dss = [], []
            for (first, n), s, dp in zip(query_blocks(seq), scores, grads):
                p = jnp.exp(causal(s, first) - log_total[:, first : first + n])
                ps.append(p.astype(bf16))
                dss.append((p * (dp - jnp.sum(p * dp, axis=0, keepdims=True))).astype(bf16))
            ready.append((ps, dss))
        for (h, at_q, at_k, at_v, q, k, do, _, _), (ps, dss) in zip(todo, ready):
            dq, dk, dv = [], [], []
            for (first, n), p, ds in zip(query_blocks(seq), ps, dss):
                dq.append(nn(k[:, : first + n], ds))
                dk.append(nt(q[:, first : first + n], ds))
                dv.append(nt(do[:, first : first + n], p))
            qkv[at_q, :seq] = (jnp.concatenate(dq, axis=1) + x[at_q, :]).astype(bf16)
            qkv[at_k, :seq] = add_up(dk).astype(bf16)
            qkv[at_v, :seq] = add_up(dv).astype(bf16)

    def grad_qkv(name, first, count):
        for p in range(3):
            at = p * width + first
            val = nt(h1[...], qkv[at : at + count, :])
            for j in range(GROUP):
                v = val[j * r : (j + 1) * r]
                all_shares[f"{name}{p}"].store(j, jnp.concatenate([v[:, : count // 2], v[:, count // 2 :]], axis=0))
            all_shares[f"{name}{p}"].send()
            pump(PLAN[f"{name}{p}"])

    pairs = heads // 2
    for i in range(pairs):
        pair_back(i)
        pump(PLAN[f"pair{i}"])
        if 2 * (i + 1) == heads_a:
            grad_qkv("a", 0, cols_a)
    grad_qkv("b", cols_a, cols_b)

    loads["tokens2"].wait()
    loads["w_qkv2"].wait()
    gm = []
    for i in range(3):
        rows = slice(i * third, (i + 1) * third)
        val = nn(slot_qkv[rows, :], qkv[...])
        x[rows, :] = val[:, :seq]
        gm.append(val[:, seq:])
        pump(PLAN[f"in{i}"])
    mem_own[1] = jnp.transpose(jnp.concatenate(gm, axis=0))[:MEM].astype(bf16)
    grads = to_beside(1)
    acc_b[...] = jnp.zeros_like(acc_b)
    acc_a[...] = jnp.zeros_like(acc_a)

    def first_sums(c, carry):
        at = lanes_of(c)
        n, _ = norm_stats(jnp.transpose(dy[at, :].astype(f32)))
        u = x[:, at]
        acc_b[...] += u * n
        acc_a[...] += u
        return carry

    lax.fori_loop(0, chunks, first_sums, 0)
    small_own[0, 0:1, :] = columns_sum(acc_b)
    small_own[0, 1:2, :] = columns_sum(acc_a)
    small.send()
    pump(PLAN["sums"])

    def first_back(c, carry):
        at = lanes_of(c)
        n, inv = norm_stats(jnp.transpose(dy[at, :].astype(f32)))
        ug = x[:, at] * norms[:, 0 : 1]
        m1 = jnp.mean(ug, axis=0, keepdims=True)
        m2 = jnp.mean(ug * n, axis=0, keepdims=True)
        g[:, at] = g[:, at] + inv * (ug - m1 - n * m2)
        return carry

    lax.fori_loop(0, 3, first_back, 0)
    pump(PLAN["back0"])
    lax.fori_loop(3, chunks, first_back, 0)
    put(g, gtok_o)
    load("after", after_o, x)
    pump(PLAN["back1"])
    grads.wait()
    gcoef[me] = tn(weights_e[me], mem_own[1])
    gcoef[1 - me] = tn(weights_e[1 - me], mem_recv[1])
    put(gcoef, gcoef_o)
    pump(PLAN["coef"])
    loads["after"].wait()
    for i in range(3):
        cols = slice(i * third, (i + 1) * third)
        dy[:, cols] = jnp.transpose(x[cols, :] + tn(w_down[:, cols], act[...])).astype(bf16)
        pump(PLAN[f"mix{i}"])
    put(dy, mixed_o)
    put(s_down, s_down_o)
    pump(PLAN["end"])
    at = 0
    for p in range(3):
        part = own_u[p].shape[2]
        v = all_shares[f"u{p}"].last()
        s_up[:, at : at + part] = v[:r]
        s_up[:, half_up + at : half_up + at + part] = v[r:]
        at += part
    put(s_up, s_up_o)
    v = all_shares["o"].last()
    s_out[:, :half_o] = v[:r]
    s_out[:, half_o:] = v[r:]
    put(s_out, s_out_o)
    for p in range(3):
        for name, first, count in (("a", 0, cols_a), ("b", cols_a, cols_b)):
            at = p * width + first
            v = all_shares[f"{name}{p}"].last()
            s_qkv[:, at : at + count // 2] = v[:r]
            s_qkv[:, at + count // 2 : at + count] = v[r:]
    put(s_qkv, s_qkv_o)
    put(small_own.at[len(SMALL_ORDER)], small_o)
    for copy in puts:
        if copy is not after_put:
            copy.wait()


def run_layer(place, heads, blocks, flag, centres, widths, norms, tokens, coeffs, dy, w_qkv, w_out, w_up, w_down):
    seq, width = tokens.shape
    ff = w_up.shape[1]
    local = coeffs.shape[1]
    span = seq // blocks
    scale = 1.0 / math.sqrt(width // heads)
    r, r_d = width // GROUP, ff // GROUP
    wide = seq + LANES
    S = jax.ShapeDtypeStruct
    outs = [
        S((seq, width), bf16),
        S((width, seq), f32),
        S((2, local, width), f32),
        S((r, 3 * width), f32),
        S((r, width), f32),
        S((r, ff), f32),
        S((r_d, width), f32),
        S((8, width), f32),
        S((width, seq), f32),
    ]
    part_d = (r_d // 2, 2 * width // 3)
    unit = ff // 24
    parts_u = [(2 * r, n * unit) for n in (5, 4, 3)]
    part_o = (2 * r, width // 2)

    def vm(*shape, dtype=bf16):
        return pltpu.VMEM(shape, dtype)

    scratch = [
        vm(2, local, width),
        vm(seq, width),
        vm(width, ff),
        vm(ff, width),
        vm(width, seq, dtype=f32),
        vm(width, seq, dtype=f32),
        vm(width, wide),
        vm(3 * width, wide),
        vm(heads, 8, seq, dtype=f32),
        vm(width, seq),
        vm(width, seq),
        vm(ff, seq),
        vm(GROUP, r_d, seq),
        vm(width, seq),
        vm(2, local, width, dtype=f32),
        vm(width, LANES, dtype=f32),
        vm(width, LANES, dtype=f32),
        vm(width, LANES, dtype=f32),
        vm(MEM, seq, dtype=f32),
        vm(width, LANES),
        vm(width, LANES),
        vm(MEM, width),
        vm(2, MEM, local),
        vm(MEM, width, dtype=f32),
        vm(r, 3 * width, dtype=f32),
        vm(r, width, dtype=f32),
        vm(r, ff, dtype=f32),
        vm(r_d, width, dtype=f32),
        vm(3, GROUP, *part_d),
        vm(3, GROUP - 1, *part_d),
        *[vm(GROUP, *part) for part in parts_u],
        *[vm(GROUP - 1, *part) for part in parts_u],
        vm(GROUP, *part_o),
        vm(GROUP - 1, *part_o),
        vm(3, GROUP - 1, 2 * r, width // 6),
        vm(2, MEM, width),
        vm(2, MEM, width),
        vm(len(SMALL_ORDER) + 1, 8, width, dtype=f32),
        vm(len(PARTNERS), 8, width, dtype=f32),
        pltpu.SemaphoreType.DMA((12,)),
        pltpu.SemaphoreType.DMA((9,)),
        pltpu.SemaphoreType.DMA((14, len(PARTNERS))),
        pltpu.SemaphoreType.DMA((14, len(PARTNERS))),
        pltpu.SemaphoreType.REGULAR((3, STAGES)),
        pltpu.SemaphoreType.DMA((2, 2)),
    ]
    return pl.pallas_call(
        functools.partial(layer_kernel, place, heads, span, scale),
        out_shape=outs,
        in_specs=[SM] + [VM] * 6 + [ANY] * 7,
        out_specs=[ANY] * len(outs),
        scratch_shapes=scratch,
        compiler_params=pltpu.CompilerParams(vmem_limit_bytes=VMEM_MIB * 2**20, collective_id=0, has_side_effects=True),
    )(flag, centres, widths, *norms, tokens, coeffs, dy, w_qkv, w_out, w_up, w_down)


def hand_on(place, mixed, gtok, small, *arrays):
    width = small.shape[1]
    part = width // (place.dp * place.basis)
    count = 3 + len(arrays)

    def kernel(*refs):
        ins, outs = refs[:count], refs[count:]
        outs[0][...] = ins[0][...]
        for c in range(gtok.shape[1] // LANES):
            at = slice(c * LANES, (c + 1) * LANES)
            outs[1][at, :] = jnp.transpose(ins[1][:, at])
        flat = lax.axis_index("dp") * place.basis + lax.axis_index("basis")
        turned = pltpu.roll(ins[2][...], lax.rem(width - flat * part, width), 1)
        for i in range(4):
            outs[2 + i][...] = turned[i, :part]
        for i in range(len(arrays)):
            outs[6 + i][...] = ins[3 + i][...]

    S = jax.ShapeDtypeStruct
    shapes = [S(mixed.shape, bf16), S(gtok.shape[::-1], f32)] + [S((part,), f32)] * 4
    return pl.pallas_call(
        kernel,
        out_shape=shapes + [S(a.shape, a.dtype) for a in arrays],
        in_specs=[VM] * count,
        out_specs=[VM] * (count + 3),
        compiler_params=pltpu.CompilerParams(vmem_limit_bytes=VMEM_MIB * 2**20),
    )(mixed, gtok, small, *arrays)


def halve_rest(place, rows):
    for bit in reversed(range(place.low)):
        half = rows.shape[0] // 2
        if bit < place.basis_bits:
            axis, size, mask = "basis", place.basis, 1 << bit
        else:
            axis, size, mask = "dp", place.dp, 1 << (bit - place.basis_bits)
        mine = (lax.axis_index(axis) // mask) % 2
        keep = lax.dynamic_slice_in_dim(rows, mine * half, half, 0)
        give = lax.dynamic_slice_in_dim(rows, (1 - mine) * half, half, 0)
        rows = keep + lax.ppermute(give, axis, [(i, i ^ mask) for i in range(size)])
    return rows


def sum_rest(place, values):
    for bit in range(place.low):
        if bit < place.basis_bits:
            axis, size, mask = "basis", place.basis, 1 << bit
        else:
            axis, size, mask = "dp", place.dp, 1 << (bit - place.basis_bits)
        values = values + lax.ppermute(values, axis, [(i, i ^ mask) for i in range(size)])
    return values


def on_device(
    place,
    tokens,
    w_qkv,
    w_out,
    w_up,
    w_down,
    gain_one,
    shift_one,
    gain_two,
    shift_two,
    coeffs,
    flags,
    centres,
    widths,
    cotangent,
):
    width = tokens.shape[2]
    heads, blocks = centres.shape[1], centres.shape[2]
    norms = [gain_one, shift_one, gain_two, shift_two]
    turned = [jnp.transpose(v, (0, 2, 1)) for v in (centres, widths)]
    mixed, gtok, gcoef, *shares, small, _ = run_layer(
        place, heads, blocks, flags, *turned, norms, tokens[0], coeffs, cotangent[0], w_qkv, w_out, w_up, w_down
    )
    small = sum_rest(place, small)
    mixed, gtok, *vectors, gcoef, s_qkv, s_out, s_up, s_down = hand_on(place, mixed, gtok, small, gcoef, *shares)
    shares = [halve_rest(place, s) for s in (s_qkv, s_out, s_up, s_down)]
    return (mixed[None], gtok[None], gcoef, *shares, *vectors)


def solution(mesh):
    both = ("dp", "basis")
    held = P(both, None, None)
    memory = P("dp", None, None)
    in_specs = (held,) + (P(),) * 8 + (P("dp", "basis", None), P(both), memory, memory, held)
    out_specs = (held, held, P("dp", "basis", None)) + (P(both, None),) * 4 + (P(both),) * 4
    return jax.shard_map(
        functools.partial(on_device, Place(mesh.shape)), mesh=mesh, in_specs=in_specs, out_specs=out_specs, check_vma=False
    )
```

```python
import functools
import math

import jax
import jax.numpy as jnp
from jax import lax
from jax.experimental import pallas as pl
from jax.experimental.pallas import tpu as pltpu
from jax.sharding import PartitionSpec as P

f32 = jnp.float32
bf16 = jnp.bfloat16
eps = 1e-05
ANY = pl.BlockSpec(memory_space=pl.ANY)
VM = pl.BlockSpec(memory_space=pltpu.VMEM)
SM = pl.BlockSpec(memory_space=pltpu.SMEM)
MESH = pl.DeviceIdType.MESH
LANES = 128
MEM = 32
GROUP = 32
STAGES = 5
FORWARD_HEADS = 4


def nn(a, b):
    return jnp.dot(a, b, preferred_element_type=f32)


def nt(a, b):
    return lax.dot_general(a, b, (((1,), (1,)), ((), ())), preferred_element_type=f32)


def tn(a, b):
    return lax.dot_general(a, b, (((0,), (0,)), ((), ())), preferred_element_type=f32)


def lanes_of(c):
    return pl.ds(pl.multiple_of(c * LANES, LANES), LANES)


def rows_of(i, n):
    return pl.ds(pl.multiple_of(i * n, n), n)


def query_blocks(seq):
    wide = 256
    return [(q, min(wide, seq - q)) for q in range(0, seq, wide)]


def causal(scores, first):
    top, low = scores[:first], scores[first:]
    key = lax.broadcasted_iota(jnp.int32, low.shape, 0)
    query = lax.broadcasted_iota(jnp.int32, low.shape, 1)
    low = jnp.where(key <= query, low, -1e30)
    return low if first == 0 else jnp.concatenate([top, low], axis=0)


def norm_stats(x):
    cen = x - jnp.mean(x, axis=0, keepdims=True)
    inv = lax.rsqrt(jnp.mean(cen * cen, axis=0, keepdims=True) + eps)
    return cen * inv, inv


def own_head(shape, samples, features, head_dim):
    sample = lax.broadcasted_iota(jnp.int32, shape, samples)
    first = lax.rem(sample, 16) * head_dim
    feature = lax.broadcasted_iota(jnp.int32, shape, features)
    return (sample < MEM) & (feature >= first) & (feature < first + head_dim)


def two_parts(values):
    high = values.astype(bf16)
    low = (values - high.astype(f32)).astype(bf16)
    return jnp.concatenate([high, low, jnp.zeros((LANES - 2 * MEM, values.shape[1]), bf16)], axis=0)


def add_up(parts):
    total = parts[-1]
    for part in reversed(parts[:-1]):
        have = part.shape[1]
        total = jnp.concatenate([total[:, :have] + part, total[:, have:]], axis=1)
    return total


def ahead(count, product, use):
    have = product(0)
    for i in range(count):
        following = product(i + 1) if i + 1 < count else None
        use(i, have)
        have = following


def columns_sum(acc):
    return jnp.sum(jnp.transpose(acc[...]), axis=0, keepdims=True)


class Place:
    def __init__(self, mesh_shape):
        self.dp, self.basis = mesh_shape["dp"], mesh_shape["basis"]
        self.bits = (self.dp * self.basis).bit_length() - 1
        self.low = self.bits - STAGES
        self.basis_bits = self.basis.bit_length() - 1

    def here(self):
        self.me_dp, self.me_basis = lax.axis_index("dp"), lax.axis_index("basis")
        flat = self.me_dp * self.basis + self.me_basis
        self.mine = [lax.rem(flat // (1 << (self.low + b)), 2) for b in range(STAGES)]

    def partner(self, bits):
        to_dp, to_basis = self.me_dp, self.me_basis
        for b in bits:
            flip = 1 - 2 * self.mine[b]
            bit = self.low + b
            if bit < self.basis_bits:
                to_basis = to_basis + flip * (1 << bit)
            else:
                to_dp = to_dp + flip * (1 << (bit - self.basis_bits))
        return (to_dp, to_basis)

    def beside(self):
        return (self.me_dp, 1 - self.me_basis)

    def spot(self, block, order):
        where = 0
        for b in (b for bits in order for b in bits):
            where = 2 * where + (1 - self.mine[b] if (block >> b) & 1 else self.mine[b])
        return where

    def greet(self):
        barrier = pltpu.get_barrier_semaphore()
        for bits in PARTNERS:
            pl.semaphore_signal(barrier, inc=1, device_id=self.partner(bits), device_id_type=MESH)
        if self.low > 0:
            pl.semaphore_signal(barrier, inc=1, device_id=self.beside(), device_id_type=MESH)

    def greeted(self):
        pl.semaphore_wait(pltpu.get_barrier_semaphore(), len(PARTNERS) + (1 if self.low > 0 else 0))


PARTNERS = ((0,), (1,), (2,), (3,), (4,), (0, 2), (3, 4))
ORDERS = (((1,), (0,), (3,), (4,), (2,)), ((1,), (2,), (0,), (3,), (4,)), ((1,), (3,), (2,), (4,), (0,)))
LATE_ORDERS = (((1,), (0,), (2,), (3, 4)), ((1,), (2,), (0,), (3, 4)), ((1,), (0, 2), (3, 4)))
SMALL_ORDER = ((1,), (0, 2), (3, 4))


def flips(bits):
    return [bits] if len(bits) == 1 else [bits[1:], bits[:1], bits]


class Share:
    def __init__(self, place, order, own, recv, rows, columns, send_sem, recv_sem, ready_sem=None, before=None):
        self.place, self.order = place, order
        (self.own, row, column), (self.recv, recv_row, recv_column) = own, recv
        self.row, self.column = row, column
        self.at = (pl.ds(row, rows), pl.ds(column, columns))
        self.recv_at = (pl.ds(recv_row, rows), pl.ds(recv_column, columns))
        self.send_sem, self.recv_sem = send_sem, recv_sem
        self.ready_sem, self.before = ready_sem, before
        self.stage, self.sent, self.left = 0, 0, GROUP
        self.all_copies = []

    def store(self, block, value, first=0):
        rows, columns = value.shape
        at = (pl.ds(self.row, rows), pl.ds(self.column + first, columns))
        self.own[(self.place.spot(block, self.order), *at)] = value.astype(bf16)

    def send(self):
        self.part = self.left >> len(self.order[self.stage])
        self.copies = []
        for i, bits in enumerate(flips(self.order[self.stage])):
            if self.before is not None:
                pl.semaphore_wait(self.before.ready_sem.at[self.stage], 1)
            copy = pltpu.make_async_remote_copy(
                src_ref=self.own.at[(pl.ds((i + 1) * self.part, self.part), *self.at)],
                dst_ref=self.recv.at[(pl.ds(GROUP - self.left + i * self.part, self.part), *self.recv_at)],
                send_sem=self.send_sem.at[self.sent],
                recv_sem=self.recv_sem.at[self.sent],
                device_id=self.place.partner(bits),
                device_id_type=MESH,
            )
            copy.start()
            self.sent += 1
            self.copies.append(copy)
        self.all_copies += self.copies

    def tell(self, stage):
        if self.ready_sem is not None:
            to = self.place.partner(self.order[stage])
            pl.semaphore_signal(self.ready_sem.at[stage], inc=1, device_id=to, device_id_type=MESH)

    def pump(self):
        for copy in self.copies:
            copy.wait_recv()
        part, first, count = self.part, GROUP - self.left, len(self.copies)
        self.stage += 1
        if self.stage == len(self.order):
            for copy in self.all_copies:
                copy.wait_send()
            return

        def add(k, carry):
            here = (k, *self.at)
            total = self.own[here]
            for i in range(count):
                total = total + self.recv[(first + i * part + k, *self.recv_at)]
            self.own[here] = total
            return carry

        lax.fori_loop(0, part, add, 0, unroll=min(4, part))
        self.left = part
        self.tell(self.stage - 1)
        self.send()

    def done(self):
        return self.stage == len(self.order)

    def last(self):
        total = self.own[(0, *self.at)].astype(f32)
        for i in range(len(self.copies)):
            total = total + self.recv[(GROUP - self.left + i, *self.recv_at)].astype(f32)
        self.tell(len(self.order) - 1)
        return total


class Whole:
    def __init__(self, place, order, own, recv, send_sem, recv_sem):
        self.place, self.order, self.own, self.recv = place, order, own, recv
        self.send_sem, self.recv_sem = send_sem, recv_sem
        self.stage, self.sent = 0, 0

    def send(self):
        self.copies = []
        for bits in flips(self.order[self.stage]):
            copy = pltpu.make_async_remote_copy(
                src_ref=self.own.at[self.stage],
                dst_ref=self.recv.at[self.sent],
                send_sem=self.send_sem.at[self.sent],
                recv_sem=self.recv_sem.at[self.sent],
                device_id=self.place.partner(bits),
                device_id_type=MESH,
            )
            copy.start()
            self.sent += 1
            self.copies.append(copy)

    def pump(self):
        total = self.own[self.stage]
        for i, copy in enumerate(self.copies):
            copy.wait()
            total = total + self.recv[self.sent - len(self.copies) + i]
        self.stage += 1
        self.own[self.stage] = total
        if not self.done():
            self.send()

    def done(self):
        return self.stage == len(self.order)


VMEM_MIB = 63
PLAN = {
    "down0": (),
    "down1": (),
    "down2": (),
    "pre0": ("d0",),
    "pre1": ("d1", "d2"),
    "pre2": (),
    "pre3": (),
    "up0": (),
    "up1": (),
    "up2": (),
    "hid0": ("u0", "d0", "u1", "u2", "d1"),
    "hid1": ("d2",),
    "hid2": (),
    "norm2": (),
    "out": (),
    "att": (),
    "pair0": ("d0", "o", "d1", "u2", "d2"),
    "pair1": (),
    "pair2": ("u1", "u0", "d1"),
    "pair3": (),
    "a0": (),
    "a1": (),
    "a2": ("a0", "u2"),
    "pair4": ("a1", "u1", "a2", "d0", "u0", "o"),
    "pair5": ("d1", "d2"),
    "b0": (),
    "b1": (),
    "b2": ("d0",),
    "in0": ("b0", "a0", "b1", "b2", "u1", "u2", "d2", "a1"),
    "in1": ("o", "a2"),
    "in2": ("b1", "a0"),
    "sums": ("u0", "u2", "o", "u1", "a2"),
    "back0": ("s",),
    "back1": ("b0", "u0", "a0", "b2", "b1", "a1"),
    "coef": (),
    "mix0": ("s", "o", "a0"),
    "mix1": ("b0", "a1", "a2"),
    "mix2": ("b2", "b1"),
    "end": ("a2", "s", "b0", "a1"),
}


def layer_kernel(
    place,
    heads,
    span,
    scale,
    flag,
    centres,
    widths,
    gain_one,
    shift_one,
    gain_two,
    shift_two,
    tokens_h,
    coeffs_h,
    dy_h,
    w_qkv_h,
    w_out_h,
    w_up_h,
    w_down_h,
    mixed_o,
    gtok_o,
    gcoef_o,
    s_qkv_o,
    s_out_o,
    s_up_o,
    s_down_o,
    small_o,
    after_o,
    coeffs,
    dy,
    w_slot,
    w_down,
    x,
    g,
    h1,
    qkv,
    aux,
    joined,
    h2,
    act,
    slope,
    da,
    gcoef,
    acc_a,
    acc_b,
    norms,
    sig,
    k_dup,
    v_dup,
    v_rows,
    weights_e,
    mem_keep,
    s_qkv,
    s_out,
    s_up,
    s_down,
    own_d,
    recv_d,
    own_u0,
    own_u1,
    own_u2,
    recv_u0,
    recv_u1,
    recv_u2,
    own_o,
    recv_o,
    recv_b,
    mem_own,
    mem_recv,
    small_own,
    small_recv,
    load_sem,
    put_sem,
    send_sem,
    recv_sem,
    ready_sem,
    mem_sem,
):
    seq, width = dy.shape
    ff = act.shape[0]
    hd = width // heads
    chunks = seq // LANES
    r, r_d = width // GROUP, ff // GROUP
    third = width // 3
    place.here()
    me = place.me_basis
    loads, puts = {}, []

    def load(name, src, dst):
        loads[name] = pltpu.make_async_copy(src, dst, load_sem.at[len(loads)])
        loads[name].start()

    def put(src, dst):
        copy = pltpu.make_async_copy(src, dst, put_sem.at[len(puts)])
        copy.start()
        puts.append(copy)
        return copy

    slot_qkv, slot_out = w_slot.at[:, pl.ds(0, 3 * width)], w_slot.at[:, pl.ds(3 * width, width)]
    load("tokens", tokens_h, dy)
    load("coeffs", coeffs_h, coeffs)
    load("w_qkv", w_qkv_h, slot_qkv)
    place.greet()
    load("w_out", w_out_h, slot_out)
    load("w_down", w_down_h, w_down)

    given = [ref[...].reshape(1, width) for ref in (gain_one, shift_one, gain_two, shift_two)]
    norms[...] = jnp.transpose(jnp.concatenate(given + [jnp.zeros((LANES - 4, width), f32)], axis=0))

    local = coeffs.shape[1]
    place_of = me * local + lax.broadcasted_iota(jnp.int32, (MEM, local), 1)
    near = lax.broadcasted_iota(jnp.int32, (16, LANES), 0) == lax.broadcasted_iota(jnp.int32, (16, LANES), 1)

    def upright(ref, s):
        parts = []
        for b in range(2):
            row = jnp.concatenate([ref[s, b : b + 1, :], jnp.zeros((1, LANES - heads), jnp.int32)], axis=1).astype(f32)
            parts.append(jnp.sum(jnp.where(near, row, 0.0), axis=1, keepdims=True))
        return jnp.concatenate(parts, axis=0)

    row_id = lax.broadcasted_iota(jnp.int32, (MEM, local), 0)
    real = lax.rem(row_id, 16) < heads
    for s in range(2):
        c, w = upright(centres, s), upright(widths, s)
        spread = w * w + 4.0
        gap = c - place_of.astype(f32)
        value = 2.0 * lax.rsqrt(spread) * jnp.exp(-gap * gap / (2.0 * spread))
        weights_e[s] = jnp.where(real, value, 0.0).astype(bf16)
    loads["coeffs"].wait()
    mem_own[0] = nn(weights_e[1 - me], coeffs[1 - me]).astype(bf16)
    place.greeted()

    def to_beside(i):
        copy = pltpu.make_async_remote_copy(
            src_ref=mem_own.at[i],
            dst_ref=mem_recv.at[i],
            send_sem=mem_sem.at[i, 0],
            recv_sem=mem_sem.at[i, 1],
            device_id=place.beside(),
            device_id_type=MESH,
        )
        copy.start()
        return copy

    samples = to_beside(0)
    mem_keep[...] = nn(weights_e[me], coeffs[me])

    loads["tokens"].wait()

    def enter(c, carry):
        at = lanes_of(c)
        v = jnp.transpose(dy[at, :].astype(f32))
        x[:, at] = v
        n, _ = norm_stats(v)
        h1[:, at] = (n * norms[:, 0 : 1] + norms[:, 1 : 2]).astype(bf16)
        return carry

    lax.fori_loop(0, chunks, enter, 0, unroll=True)
    load("dy", dy_h, dy)
    loads["w_qkv"].wait()
    half_w = width // 2
    for i in range(2):
        at = i * half_w
        qkv[at : at + half_w, :seq] = tn(slot_qkv[:, at : at + half_w], h1[:, :seq]).astype(bf16)
    samples.wait()
    memory = (mem_keep[...] + mem_recv[0].astype(f32)).astype(bf16).astype(f32)
    memory = jnp.concatenate([memory, jnp.zeros((LANES - MEM, width), f32)], axis=0)
    h1[:, seq:] = jnp.transpose(memory).astype(bf16)

    def project(i):
        at = (i + 2) * half_w
        return tn(slot_qkv[:, at : at + half_w], h1[...])

    def keep_projected(i, value):
        at = (i + 2) * half_w
        qkv[at : at + half_w, :] = value.astype(bf16)

    ahead(4, project, keep_projected)
    load("w_up_a", w_up_h.at[:, pl.ds(0, 3 * width)], slot_qkv)
    on = flag[0].astype(f32)
    own_column = own_head((width, LANES), 1, 0, hd)
    mem_part = pl.ds(seq, LANES)
    in_block = lax.broadcasted_iota(jnp.int32, (MEM, seq), 0) // 16 == lax.broadcasted_iota(jnp.int32, (MEM, seq), 1) // span
    for i, dup, rows in ((1, k_dup, None), (2, v_dup, v_rows)):
        wide = jnp.where(own_column, qkv[i * width : (i + 1) * width, mem_part].astype(f32), 0.0)
        dup[...] = (wide + pltpu.roll(wide, MEM, 1)).astype(bf16)
        turned = jnp.transpose(wide)[:MEM]
        if rows is None:
            score = nn((turned * scale).astype(bf16), qkv[:width, :seq])
        else:
            rows[...] = turned.astype(bf16)
    sig[...] = jnp.where(in_block, jax.nn.sigmoid(score), 0.0)
    g[...] = nn(v_dup[...], two_parts(sig[...] * on))

    def heads_forward(i, carry):
        def scores(j):
            h = i * FORWARD_HEADS + j
            base = pl.multiple_of(h * hd, hd)
            q = qkv[pl.ds(base, hd), :seq] * jnp.asarray(scale, bf16)
            k = jnp.transpose(qkv[pl.ds(width + base, hd), :seq])
            return h, base, [nn(k[: first + n], q[:, first : first + n]) for first, n in query_blocks(seq)]

        def use(j, given):
            h, base, products = given
            weights, totals, logs = [], [], []
            for (first, n), s in zip(query_blocks(seq), products):
                s = causal(s, first)
                peak = jnp.max(s, axis=0, keepdims=True)
                e = jnp.exp(s - peak)
                weights.append(e.astype(bf16))
                totals.append(jnp.sum(e, axis=0, keepdims=True))
                logs.append(peak + jnp.log(totals[-1]))
            v = qkv[pl.ds(2 * width + base, hd), :seq]
            o = [nn(v[:, : e.shape[0]], e) / total for e, total in zip(weights, totals)]
            joined[pl.ds(base, hd), :] = (jnp.concatenate(o, axis=1) + g[pl.ds(base, hd), :]).astype(bf16)
            aux[h] = jnp.broadcast_to(jnp.concatenate(logs, axis=1), (8, seq))

        ahead(FORWARD_HEADS, scores, use)
        return carry

    lax.fori_loop(0, heads // FORWARD_HEADS, heads_forward, 0)
    loads["w_out"].wait()
    x[...] = x[...] + tn(slot_out[...], joined[...])
    load("w_up_b", w_up_h.at[:, pl.ds(3 * width, width)], slot_out)
    after_put = put(x, after_o)

    def second(c, carry):
        at = lanes_of(c)
        n, _ = norm_stats(x[:, at])
        h2[:, at] = (n * norms[:, 2 : 3] + norms[:, 3 : 4]).astype(bf16)
        return carry

    lax.fori_loop(0, chunks, second, 0, unroll=True)
    loads["w_up_a"].wait()
    step = 384

    def up_product(i):
        if i * step == 3 * width:
            loads["w_up_b"].wait()
        return tn(w_slot[:, i * step : (i + 1) * step], h2[...])

    def up_use(i, pre):
        sq = pre * pre
        c = math.sqrt(2.0 / math.pi)
        t = jnp.tanh(pre * (c + (c * 0.044715) * sq))
        half = 0.5 + 0.5 * t
        act[i * step : (i + 1) * step, :] = (pre * half).astype(bf16)
        rate = half + (0.5 * pre) * (1.0 - t * t) * (c + (3 * c * 0.044715) * sq)
        slope[i * step // r_d : (i + 1) * step // r_d] = rate.astype(bf16).reshape(step // r_d, r_d, seq)

    ahead(ff // step, up_product, up_use)

    half_d = r_d // 2
    all_shares = {}
    rows_o, columns_o = own_o.shape[1:]
    rows_d, columns_d = own_d.shape[2:]
    own_u, recv_u = (own_u0, own_u1, own_u2), (recv_u0, recv_u1, recv_u2)
    heads_a = heads * 2 // 3
    cols_a, cols_b = heads_a * hd, (heads - heads_a) * hd
    a, b = cols_a // 2, cols_b // 2

    def share(name, p, *where, orders=ORDERS, **more):
        i = len(all_shares)
        all_shares[name] = Share(place, orders[p], *where, send_sem.at[i], recv_sem.at[i], **more)

    for p in range(3):
        share(f"d{p}", p, (own_d.at[p], 0, 0), (recv_d.at[p], 0, 0), rows_d, columns_d, ready_sem=ready_sem.at[p])
    for p in range(3):
        share(f"u{p}", p, (own_u[p], 0, 0), (recv_u[p], 0, 0), *own_u[p].shape[1:])
    share("o", 1, (own_o, 0, 0), (recv_o, 0, 0), rows_o, columns_o)
    spots = {"a": ((0, 0), (0, a), (rows_o, 0)), "b": ((0, 2 * a), (rows_o, a), (rows_o, a + b))}
    for p in range(3):
        before = all_shares[f"d{p}"]
        share(f"a{p}", p, (slope, *spots["a"][p]), (recv_d.at[p], 0, 0), rows_o, a, before=before)
    for p in range(3):
        share(f"b{p}", p, (slope, *spots["b"][p]), (recv_b.at[p], 0, 0), rows_o, b, orders=LATE_ORDERS)
    small = Whole(place, SMALL_ORDER, small_own, small_recv, send_sem.at[13], recv_sem.at[13])
    all_shares["s"] = small

    def pump(names):
        for name in names:
            all_shares[name].pump()
            if name[0] == "d" and all_shares[name].done():
                v, p = all_shares[name].last(), int(name[1])
                s_down[:half_d, p * third : (p + 1) * third] = v[:, :third]
                s_down[half_d:, p * third : (p + 1) * third] = v[:, third:]

    loads["dy"].wait()
    blocks = GROUP // 4

    def down_product(i):
        p, piece = i // 4, i % 4
        return nn(act[piece * blocks * r_d : (piece + 1) * blocks * r_d, :], dy[:, p * third : (p + 1) * third])

    def down_use(i, val):
        p, piece = i // 4, i % 4
        for j in range(blocks):
            v = val[j * r_d : (j + 1) * r_d]
            all_shares[f"d{p}"].store(piece * blocks + j, jnp.concatenate([v[:half_d], v[half_d:]], axis=1))
        if piece == 3:
            all_shares[f"d{p}"].send()
            pump(PLAN[f"down{p}"])

    ahead(12, down_product, down_use)
    loads["w_down"].wait()

    def pre_product(i):
        return nt(w_down[i * step : (i + 1) * step, :], dy[...])

    def pre_use(i, val):
        at = slice(i * step // r_d, (i + 1) * step // r_d)
        rate = slope[at].reshape(step, seq).astype(f32)
        slope[at] = (val * rate).astype(bf16).reshape(step // r_d, r_d, seq)
        if i % 2 == 1:
            pump(PLAN[f"pre{i // 2}"])

    ahead(ff // step, pre_product, pre_use)
    half_up = ff // 2

    def slope_rows(first, count):
        low, high = first // r_d, -(-(first + count) // r_d)
        rows = slope[low:high].reshape((high - low) * r_d, seq)
        return rows[first - low * r_d : first - low * r_d + count]

    pieces, at = [], 0
    for p in range(3):
        part = own_u[p].shape[2]
        for sub in range(0, part, 256):
            count = min(256, part - sub)
            pieces.append((p, sub, at, count, sub + count == part))
            at += count

    def up_grad(i):
        _, _, at, count, _ = pieces[i]
        return nt(h2[...], slope_rows(at, count)), nt(h2[...], slope_rows(half_up + at, count))

    def up_grad_use(i, val):
        (p, sub, _, _, ends), (left, right) = pieces[i], val
        for j in range(GROUP):
            rows = slice(j * r, (j + 1) * r)
            all_shares[f"u{p}"].store(j, jnp.concatenate([left[rows], right[rows]], axis=0), sub)
        if ends:
            all_shares[f"u{p}"].send()
            pump(PLAN[f"up{p}"])

    ahead(len(pieces), up_grad, up_grad_use)
    for i in range(3):
        rows = slice(i * third, (i + 1) * third)
        g[rows, :] = nn(w_slot[rows, :], slope[...].reshape(ff, seq))
        pump(PLAN[f"hid{i}"])
    load("w_qkv2", w_qkv_h, slot_qkv)
    load("w_out2", w_out_h, slot_out)

    acc_b[...] = jnp.zeros_like(acc_b)
    acc_a[...] = jnp.zeros_like(acc_a)

    def second_back(c, carry):
        at = lanes_of(c)
        n, inv = norm_stats(x[:, at])
        u = g[:, at]
        un = u * n
        acc_b[...] += un
        acc_a[...] += u
        ug = u * norms[:, 2 : 3]
        m1 = jnp.mean(ug, axis=0, keepdims=True)
        m2 = jnp.mean(un * norms[:, 2 : 3], axis=0, keepdims=True)
        v = jnp.transpose(dy[at, :].astype(f32)) + inv * (ug - m1 - n * m2)
        g[:, at] = v
        da[:, at] = v.astype(bf16)
        return carry

    lax.fori_loop(0, chunks, second_back, 0, unroll=True)
    load("tokens2", tokens_h, dy)
    small_own[0, 2:3, :] = columns_sum(acc_b)
    small_own[0, 3:4, :] = columns_sum(acc_a)
    small_own[0, 4:8, :] = jnp.zeros((4, width), f32)
    pump(PLAN["norm2"])
    half_o = width // 2
    left, right = nt(joined[...], da[:half_o, :]), nt(joined[...], da[half_o:, :])
    for j in range(GROUP):
        rows = slice(j * r, (j + 1) * r)
        all_shares["o"].store(j, jnp.concatenate([left[rows], right[rows]], axis=0))
    all_shares["o"].send()
    pump(PLAN["out"])
    loads["w_out2"].wait()
    datt = h2
    datt[...] = nn(slot_out[...], da[...]).astype(bf16)
    pump(PLAN["att"])

    gates = sig[...]
    dscore = two_parts((on * scale) * nn(v_rows[...], datt[...]) * gates * (1.0 - gates))
    after_put.wait()
    x[...] = nn(k_dup[...], dscore)
    for i, wide in ((1, nt(qkv[:width, :seq], dscore)), (2, nt(datt[...], two_parts(gates * on)))):
        total = wide + pltpu.roll(wide, LANES - MEM, 1)
        qkv[i * width : (i + 1) * width, mem_part] = jnp.where(own_column, total, 0.0).astype(bf16)
    qkv[:width, mem_part] = jnp.zeros((width, LANES), bf16)

    def pair_back(i):
        todo = []
        for h in (2 * i, 2 * i + 1):
            at_q, at_k, at_v = (slice(j * width + h * hd, j * width + (h + 1) * hd) for j in range(3))
            q = qkv[at_q, :seq] * jnp.asarray(scale, bf16)
            k = qkv[at_k, :seq]
            k_up, v_up = jnp.transpose(k), jnp.transpose(qkv[at_v, :seq])
            do = datt[at_q, :]
            s = [nn(k_up[: first + n], q[:, first : first + n]) for first, n in query_blocks(seq)]
            dp = [nn(v_up[: first + n], do[:, first : first + n]) for first, n in query_blocks(seq)]
            todo.append((h, at_q, at_k, at_v, q, k * jnp.asarray(scale, bf16), do, s, dp))
        ready = []
        for h, at_q, at_k, at_v, q, k, do, scores, grads in todo:
            log_total = aux[h, 0:1, :]
            ps, dss = [], []
            for (first, n), s, dp in zip(query_blocks(seq), scores, grads):
                p = jnp.exp(causal(s, first) - log_total[:, first : first + n])
                ps.append(p.astype(bf16))
                dss.append((p * (dp - jnp.sum(p * dp, axis=0, keepdims=True))).astype(bf16))
            ready.append((ps, dss))
        for (h, at_q, at_k, at_v, q, k, do, _, _), (ps, dss) in zip(todo, ready):
            dq, dk, dv = [], [], []
            for (first, n), p, ds in zip(query_blocks(seq), ps, dss):
                dq.append(nn(k[:, : first + n], ds))
                dk.append(nt(q[:, first : first + n], ds))
                dv.append(nt(do[:, first : first + n], p))
            qkv[at_q, :seq] = (jnp.concatenate(dq, axis=1) + x[at_q, :]).astype(bf16)
            qkv[at_k, :seq] = add_up(dk).astype(bf16)
            qkv[at_v, :seq] = add_up(dv).astype(bf16)

    def grad_qkv(name, first, count):
        for p in range(3):
            at = p * width + first
            val = nt(h1[...], qkv[at : at + count, :])
            for j in range(GROUP):
                v = val[j * r : (j + 1) * r]
                all_shares[f"{name}{p}"].store(j, jnp.concatenate([v[:, : count // 2], v[:, count // 2 :]], axis=0))
            all_shares[f"{name}{p}"].send()
            pump(PLAN[f"{name}{p}"])

    pairs = heads // 2
    for i in range(pairs):
        pair_back(i)
        pump(PLAN[f"pair{i}"])
        if 2 * (i + 1) == heads_a:
            grad_qkv("a", 0, cols_a)
    grad_qkv("b", cols_a, cols_b)

    loads["tokens2"].wait()
    loads["w_qkv2"].wait()
    gm = []
    for i in range(3):
        rows = slice(i * third, (i + 1) * third)
        val = nn(slot_qkv[rows, :], qkv[...])
        x[rows, :] = val[:, :seq]
        gm.append(val[:, seq:])
        pump(PLAN[f"in{i}"])
    mem_own[1] = jnp.transpose(jnp.concatenate(gm, axis=0))[:MEM].astype(bf16)
    grads = to_beside(1)
    acc_b[...] = jnp.zeros_like(acc_b)
    acc_a[...] = jnp.zeros_like(acc_a)

    def first_sums(c, carry):
        at = lanes_of(c)
        n, inv = norm_stats(jnp.transpose(dy[at, :].astype(f32)))
        u = x[:, at]
        un = u * n
        acc_b[...] += un
        acc_a[...] += u
        joined[:, at] = n.astype(bf16)
        m1 = jnp.mean(u * norms[:, 0:1], axis=0, keepdims=True)
        m2 = jnp.mean(un * norms[:, 0:1], axis=0, keepdims=True)
        sig[0:8, at] = jnp.concatenate([inv, m1, m2, jnp.zeros((5, LANES), f32)], axis=0)
        return carry

    lax.fori_loop(0, chunks, first_sums, 0, unroll=True)
    small_own[0, 0:1, :] = columns_sum(acc_b)
    small_own[0, 1:2, :] = columns_sum(acc_a)
    small.send()
    pump(PLAN["sums"])

    def first_back(c, carry):
        at = lanes_of(c)
        inv, m1, m2 = sig[0:1, at], sig[1:2, at], sig[2:3, at]
        n = joined[:, at].astype(f32)
        g[:, at] = g[:, at] + inv * (x[:, at] * norms[:, 0:1] - m1 - n * m2)
        return carry

    lax.fori_loop(0, 3, first_back, 0, unroll=True)
    pump(PLAN["back0"])
    lax.fori_loop(3, chunks, first_back, 0, unroll=True)
    put(g, gtok_o)
    load("after", after_o, x)
    pump(PLAN["back1"])
    grads.wait()
    gcoef[me] = tn(weights_e[me], mem_own[1])
    gcoef[1 - me] = tn(weights_e[1 - me], mem_recv[1])
    put(gcoef, gcoef_o)
    pump(PLAN["coef"])
    loads["after"].wait()
    for i in range(3):
        cols = slice(i * third, (i + 1) * third)
        dy[:, cols] = jnp.transpose(x[cols, :] + tn(w_down[:, cols], act[...])).astype(bf16)
        pump(PLAN[f"mix{i}"])
    put(dy, mixed_o)
    put(s_down, s_down_o)
    pump(PLAN["end"])
    at = 0
    for p in range(3):
        part = own_u[p].shape[2]
        v = all_shares[f"u{p}"].last()
        s_up[:, at : at + part] = v[:r]
        s_up[:, half_up + at : half_up + at + part] = v[r:]
        at += part
    put(s_up, s_up_o)
    v = all_shares["o"].last()
    s_out[:, :half_o] = v[:r]
    s_out[:, half_o:] = v[r:]
    put(s_out, s_out_o)
    for p in range(3):
        for name, first, count in (("a", 0, cols_a), ("b", cols_a, cols_b)):
            at = p * width + first
            v = all_shares[f"{name}{p}"].last()
            s_qkv[:, at : at + count // 2] = v[:r]
            s_qkv[:, at + count // 2 : at + count] = v[r:]
    put(s_qkv, s_qkv_o)
    put(small_own.at[len(SMALL_ORDER)], small_o)
    for copy in puts:
        if copy is not after_put:
            copy.wait()


def run_layer(place, heads, blocks, flag, centres, widths, norms, tokens, coeffs, dy, w_qkv, w_out, w_up, w_down):
    seq, width = tokens.shape
    ff = w_up.shape[1]
    local = coeffs.shape[1]
    span = seq // blocks
    scale = 1.0 / math.sqrt(width // heads)
    r, r_d = width // GROUP, ff // GROUP
    wide = seq + LANES
    S = jax.ShapeDtypeStruct
    outs = [
        S((seq, width), bf16),
        S((width, seq), f32),
        S((2, local, width), f32),
        S((r, 3 * width), f32),
        S((r, width), f32),
        S((r, ff), f32),
        S((r_d, width), f32),
        S((8, width), f32),
        S((width, seq), f32),
    ]
    part_d = (r_d // 2, 2 * width // 3)
    unit = ff // 24
    parts_u = [(2 * r, n * unit) for n in (5, 4, 3)]
    part_o = (2 * r, width // 2)

    def vm(*shape, dtype=bf16):
        return pltpu.VMEM(shape, dtype)

    scratch = [
        vm(2, local, width),
        vm(seq, width),
        vm(width, ff),
        vm(ff, width),
        vm(width, seq, dtype=f32),
        vm(width, seq, dtype=f32),
        vm(width, wide),
        vm(3 * width, wide),
        vm(heads, 8, seq, dtype=f32),
        vm(width, seq),
        vm(width, seq),
        vm(ff, seq),
        vm(GROUP, r_d, seq),
        vm(width, seq),
        vm(2, local, width, dtype=f32),
        vm(width, LANES, dtype=f32),
        vm(width, LANES, dtype=f32),
        vm(width, LANES, dtype=f32),
        vm(MEM, seq, dtype=f32),
        vm(width, LANES),
        vm(width, LANES),
        vm(MEM, width),
        vm(2, MEM, local),
        vm(MEM, width, dtype=f32),
        vm(r, 3 * width, dtype=f32),
        vm(r, width, dtype=f32),
        vm(r, ff, dtype=f32),
        vm(r_d, width, dtype=f32),
        vm(3, GROUP, *part_d),
        vm(3, GROUP - 1, *part_d),
        *[vm(GROUP, *part) for part in parts_u],
        *[vm(GROUP - 1, *part) for part in parts_u],
        vm(GROUP, *part_o),
        vm(GROUP - 1, *part_o),
        vm(3, GROUP - 1, 2 * r, width // 6),
        vm(2, MEM, width),
        vm(2, MEM, width),
        vm(len(SMALL_ORDER) + 1, 8, width, dtype=f32),
        vm(len(PARTNERS), 8, width, dtype=f32),
        pltpu.SemaphoreType.DMA((12,)),
        pltpu.SemaphoreType.DMA((9,)),
        pltpu.SemaphoreType.DMA((14, len(PARTNERS))),
        pltpu.SemaphoreType.DMA((14, len(PARTNERS))),
        pltpu.SemaphoreType.REGULAR((3, STAGES)),
        pltpu.SemaphoreType.DMA((2, 2)),
    ]
    return pl.pallas_call(
        functools.partial(layer_kernel, place, heads, span, scale),
        out_shape=outs,
        in_specs=[SM] + [VM] * 6 + [ANY] * 7,
        out_specs=[ANY] * len(outs),
        scratch_shapes=scratch,
        compiler_params=pltpu.CompilerParams(vmem_limit_bytes=VMEM_MIB * 2**20, collective_id=0, has_side_effects=True),
    )(flag, centres, widths, *norms, tokens, coeffs, dy, w_qkv, w_out, w_up, w_down)


def hand_on(place, mixed, gtok, small, *arrays):
    width = small.shape[1]
    part = width // (place.dp * place.basis)
    count = 3 + len(arrays)

    def kernel(*refs):
        ins, outs, vectors = refs[:count], refs[count : 2 * count - 1], refs[2 * count - 1 : 2 * count + 3]
        held, parts = refs[2 * count + 3 : 3 * count + 3], refs[3 * count + 3 : 3 * count + 7]
        upright, in_sem, out_sem = refs[3 * count + 7 :]
        coming = [pltpu.make_async_copy(ins[i], held[i], in_sem.at[i]) for i in range(count)]
        leaving = []

        def leave(src, dst):
            leaving.append(pltpu.make_async_copy(src, dst, out_sem.at[len(leaving)]))
            leaving[-1].start()

        for copy in coming:
            copy.start()
        coming[0].wait()
        for c in range(gtok.shape[1] // LANES):
            at = slice(c * LANES, (c + 1) * LANES)
            upright[at, :] = jnp.transpose(held[0][:, at])
            leave(upright.at[at, :], outs[0].at[at, :])
        for i in range(1, count - 1):
            coming[i].wait()
            leave(held[i], outs[i])
        coming[-1].wait()
        flat = lax.axis_index("dp") * place.basis + lax.axis_index("basis")
        turned = pltpu.roll(held[-1][...], lax.rem(width - flat * part, width), 1)
        for i in range(4):
            parts[i][...] = turned[i, :part]
            leave(parts[i], vectors[i])
        for copy in leaving:
            copy.wait()

    S = jax.ShapeDtypeStruct
    arrays = (gtok, mixed, *arrays, small)
    shapes = [S(gtok.shape[::-1], f32)] + [S(a.shape, a.dtype) for a in arrays[1:-1]]
    return pl.pallas_call(
        kernel,
        out_shape=shapes + [S((part,), f32)] * 4,
        in_specs=[ANY] * count,
        out_specs=[ANY] * (count + 3),
        scratch_shapes=[pltpu.VMEM(a.shape, a.dtype) for a in arrays]
        + [pltpu.VMEM((part,), f32)] * 4
        + [pltpu.VMEM(gtok.shape[::-1], f32)]
        + [pltpu.SemaphoreType.DMA((count,)), pltpu.SemaphoreType.DMA((count + 2 + gtok.shape[1] // LANES,))],
        compiler_params=pltpu.CompilerParams(vmem_limit_bytes=VMEM_MIB * 2**20),
    )(*arrays)


def halve_rest(place, rows):
    for bit in reversed(range(place.low)):
        half = rows.shape[0] // 2
        if bit < place.basis_bits:
            axis, size, mask = "basis", place.basis, 1 << bit
        else:
            axis, size, mask = "dp", place.dp, 1 << (bit - place.basis_bits)
        mine = (lax.axis_index(axis) // mask) % 2
        keep = lax.dynamic_slice_in_dim(rows, mine * half, half, 0)
        give = lax.dynamic_slice_in_dim(rows, (1 - mine) * half, half, 0)
        rows = keep + lax.ppermute(give, axis, [(i, i ^ mask) for i in range(size)])
    return rows


def sum_rest(place, values):
    for bit in range(place.low):
        if bit < place.basis_bits:
            axis, size, mask = "basis", place.basis, 1 << bit
        else:
            axis, size, mask = "dp", place.dp, 1 << (bit - place.basis_bits)
        values = values + lax.ppermute(values, axis, [(i, i ^ mask) for i in range(size)])
    return values


def on_device(
    place,
    tokens,
    w_qkv,
    w_out,
    w_up,
    w_down,
    gain_one,
    shift_one,
    gain_two,
    shift_two,
    coeffs,
    flags,
    centres,
    widths,
    cotangent,
):
    width = tokens.shape[2]
    heads, blocks = centres.shape[1], centres.shape[2]
    norms = [gain_one, shift_one, gain_two, shift_two]
    turned = [jnp.transpose(v, (0, 2, 1)) for v in (centres, widths)]
    mixed, gtok, gcoef, *shares, small, _ = run_layer(
        place, heads, blocks, flags, *turned, norms, tokens[0], coeffs, cotangent[0], w_qkv, w_out, w_up, w_down
    )
    small = sum_rest(place, small)
    gtok, mixed, gcoef, s_qkv, s_out, s_up, s_down, *vectors = hand_on(place, mixed, gtok, small, gcoef, *shares)
    shares = [halve_rest(place, s) for s in (s_qkv, s_out, s_up, s_down)]
    return (mixed[None], gtok[None], gcoef, *shares, *vectors)


def solution(mesh):
    both = ("dp", "basis")
    held = P(both, None, None)
    memory = P("dp", None, None)
    in_specs = (held,) + (P(),) * 8 + (P("dp", "basis", None), P(both), memory, memory, held)
    out_specs = (held, held, P("dp", "basis", None)) + (P(both, None),) * 4 + (P(both),) * 4
    return jax.shard_map(
        functools.partial(on_device, Place(mesh.shape)), mesh=mesh, in_specs=in_specs, out_specs=out_specs, check_vma=False
    )
```

```python
import functools
import math

import jax
import jax.numpy as jnp
from jax import lax
from jax.experimental import pallas as pl
from jax.experimental.pallas import tpu as pltpu
from jax.sharding import PartitionSpec as P

f32 = jnp.float32
bf16 = jnp.bfloat16
eps = 1e-05
ANY = pl.BlockSpec(memory_space=pl.ANY)
VM = pl.BlockSpec(memory_space=pltpu.VMEM)
SM = pl.BlockSpec(memory_space=pltpu.SMEM)
MESH = pl.DeviceIdType.MESH
LANES = 128
MEM = 32
GROUP = 32
STAGES = 5
FORWARD_HEADS = 4


def nn(a, b):
    return jnp.dot(a, b, preferred_element_type=f32)


def nt(a, b):
    return lax.dot_general(a, b, (((1,), (1,)), ((), ())), preferred_element_type=f32)


def tn(a, b):
    return lax.dot_general(a, b, (((0,), (0,)), ((), ())), preferred_element_type=f32)


def lanes_of(c):
    return pl.ds(pl.multiple_of(c * LANES, LANES), LANES)


def rows_of(i, n):
    return pl.ds(pl.multiple_of(i * n, n), n)


def query_blocks(seq):
    wide = 256
    return [(q, min(wide, seq - q)) for q in range(0, seq, wide)]


def causal(scores, first):
    top, low = scores[:first], scores[first:]
    key = lax.broadcasted_iota(jnp.int32, low.shape, 0)
    query = lax.broadcasted_iota(jnp.int32, low.shape, 1)
    low = jnp.where(key <= query, low, -1e30)
    return low if first == 0 else jnp.concatenate([top, low], axis=0)


def norm_stats(x):
    cen = x - jnp.mean(x, axis=0, keepdims=True)
    inv = lax.rsqrt(jnp.mean(cen * cen, axis=0, keepdims=True) + eps)
    return cen * inv, inv


def own_head(shape, samples, features, head_dim):
    sample = lax.broadcasted_iota(jnp.int32, shape, samples)
    first = lax.rem(sample, 16) * head_dim
    feature = lax.broadcasted_iota(jnp.int32, shape, features)
    return (sample < MEM) & (feature >= first) & (feature < first + head_dim)


def two_parts(values):
    high = values.astype(bf16)
    low = (values - high.astype(f32)).astype(bf16)
    return jnp.concatenate([high, low, jnp.zeros((LANES - 2 * MEM, values.shape[1]), bf16)], axis=0)


def add_up(parts):
    total = parts[-1]
    for part in reversed(parts[:-1]):
        have = part.shape[1]
        total = jnp.concatenate([total[:, :have] + part, total[:, have:]], axis=1)
    return total


def ahead(count, product, use):
    have = product(0)
    for i in range(count):
        following = product(i + 1) if i + 1 < count else None
        use(i, have)
        have = following


def columns_sum(acc):
    return jnp.sum(jnp.transpose(acc[...]), axis=0, keepdims=True)


class Place:
    def __init__(self, mesh_shape):
        self.dp, self.basis = mesh_shape["dp"], mesh_shape["basis"]
        self.bits = (self.dp * self.basis).bit_length() - 1
        self.low = self.bits - STAGES
        self.basis_bits = self.basis.bit_length() - 1

    def here(self):
        self.me_dp, self.me_basis = lax.axis_index("dp"), lax.axis_index("basis")
        flat = self.me_dp * self.basis + self.me_basis
        self.mine = [lax.rem(flat // (1 << (self.low + b)), 2) for b in range(STAGES)]

    def partner(self, bits):
        to_dp, to_basis = self.me_dp, self.me_basis
        for b in bits:
            flip = 1 - 2 * self.mine[b]
            bit = self.low + b
            if bit < self.basis_bits:
                to_basis = to_basis + flip * (1 << bit)
            else:
                to_dp = to_dp + flip * (1 << (bit - self.basis_bits))
        return (to_dp, to_basis)

    def beside(self):
        return (self.me_dp, 1 - self.me_basis)

    def spot(self, block, order):
        where = 0
        for b in (b for bits in order for b in bits):
            where = 2 * where + (1 - self.mine[b] if (block >> b) & 1 else self.mine[b])
        return where

    def greet(self):
        barrier = pltpu.get_barrier_semaphore()
        for bits in PARTNERS:
            pl.semaphore_signal(barrier, inc=1, device_id=self.partner(bits), device_id_type=MESH)
        if self.low > 0:
            pl.semaphore_signal(barrier, inc=1, device_id=self.beside(), device_id_type=MESH)

    def greeted(self):
        pl.semaphore_wait(pltpu.get_barrier_semaphore(), len(PARTNERS) + (1 if self.low > 0 else 0))


PARTNERS = ((0,), (1,), (2,), (3,), (4,), (0, 2), (3, 4))
ORDERS = (((1,), (0,), (3,), (4,), (2,)), ((1,), (2,), (0,), (3,), (4,)), ((1,), (3,), (2,), (4,), (0,)))
LATE_ORDERS = (((1,), (0,), (2,), (3, 4)), ((1,), (2,), (0,), (3, 4)), ((1,), (0, 2), (3, 4)))
SMALL_ORDER = ((1,), (0, 2), (3, 4))


def flips(bits):
    return [bits] if len(bits) == 1 else [bits[1:], bits[:1], bits]


class Share:
    def __init__(self, place, order, own, recv, rows, columns, send_sem, recv_sem, ready_sem=None, before=None):
        self.place, self.order = place, order
        (self.own, row, column), (self.recv, recv_row, recv_column) = own, recv
        self.row, self.column = row, column
        self.at = (pl.ds(row, rows), pl.ds(column, columns))
        self.recv_at = (pl.ds(recv_row, rows), pl.ds(recv_column, columns))
        self.send_sem, self.recv_sem = send_sem, recv_sem
        self.ready_sem, self.before = ready_sem, before
        self.stage, self.sent, self.left = 0, 0, GROUP
        self.all_copies = []

    def store(self, block, value, first=0):
        rows, columns = value.shape
        at = (pl.ds(self.row, rows), pl.ds(self.column + first, columns))
        self.own[(self.place.spot(block, self.order), *at)] = value.astype(bf16)

    def send(self):
        self.part = self.left >> len(self.order[self.stage])
        self.copies = []
        for i, bits in enumerate(flips(self.order[self.stage])):
            if self.before is not None:
                pl.semaphore_wait(self.before.ready_sem.at[self.stage], 1)
            copy = pltpu.make_async_remote_copy(
                src_ref=self.own.at[(pl.ds((i + 1) * self.part, self.part), *self.at)],
                dst_ref=self.recv.at[(pl.ds(GROUP - self.left + i * self.part, self.part), *self.recv_at)],
                send_sem=self.send_sem.at[self.sent],
                recv_sem=self.recv_sem.at[self.sent],
                device_id=self.place.partner(bits),
                device_id_type=MESH,
            )
            copy.start()
            self.sent += 1
            self.copies.append(copy)
        self.all_copies += self.copies

    def tell(self, stage):
        if self.ready_sem is not None:
            to = self.place.partner(self.order[stage])
            pl.semaphore_signal(self.ready_sem.at[stage], inc=1, device_id=to, device_id_type=MESH)

    def pump(self):
        for copy in self.copies:
            copy.wait_recv()
        part, first, count = self.part, GROUP - self.left, len(self.copies)
        self.stage += 1
        if self.stage == len(self.order):
            for copy in self.all_copies:
                copy.wait_send()
            return

        def add(k, carry):
            here = (k, *self.at)
            total = self.own[here]
            for i in range(count):
                total = total + self.recv[(first + i * part + k, *self.recv_at)]
            self.own[here] = total
            return carry

        lax.fori_loop(0, part, add, 0, unroll=min(4, part))
        self.left = part
        self.tell(self.stage - 1)
        self.send()

    def done(self):
        return self.stage == len(self.order)

    def last(self):
        total = self.own[(0, *self.at)].astype(f32)
        for i in range(len(self.copies)):
            total = total + self.recv[(GROUP - self.left + i, *self.recv_at)].astype(f32)
        self.tell(len(self.order) - 1)
        return total


class Whole:
    def __init__(self, place, order, own, recv, send_sem, recv_sem):
        self.place, self.order, self.own, self.recv = place, order, own, recv
        self.send_sem, self.recv_sem = send_sem, recv_sem
        self.stage, self.sent = 0, 0

    def send(self):
        self.copies = []
        for bits in flips(self.order[self.stage]):
            copy = pltpu.make_async_remote_copy(
                src_ref=self.own.at[self.stage],
                dst_ref=self.recv.at[self.sent],
                send_sem=self.send_sem.at[self.sent],
                recv_sem=self.recv_sem.at[self.sent],
                device_id=self.place.partner(bits),
                device_id_type=MESH,
            )
            copy.start()
            self.sent += 1
            self.copies.append(copy)

    def pump(self):
        total = self.own[self.stage]
        for i, copy in enumerate(self.copies):
            copy.wait()
            total = total + self.recv[self.sent - len(self.copies) + i]
        self.stage += 1
        self.own[self.stage] = total
        if not self.done():
            self.send()

    def done(self):
        return self.stage == len(self.order)


VMEM_MIB = 63
PLAN = {
    "down0": (),
    "down1": (),
    "down2": (),
    "pre0": ("d0",),
    "pre1": ("d1", "d2"),
    "pre2": (),
    "pre3": (),
    "up0": (),
    "up1": (),
    "up2": (),
    "hid0": ("u0", "u1", "d0", "u2", "d1"),
    "hid1": ("d2",),
    "hid2": (),
    "norm2": (),
    "out": (),
    "att": (),
    "pair0": ("o", "d0", "d1", "u2", "d2"),
    "pair1": (),
    "pair2": ("u1", "u0", "d1"),
    "pair3": (),
    "a0": (),
    "a1": (),
    "a2": ("a0", "u2"),
    "pair4": ("a1", "u1", "a2", "o", "u0"),
    "pair5": ("d0", "d1", "d2"),
    "b0": (),
    "b1": (),
    "b2": (),
    "in0": ("b0", "b1", "a0", "b2", "u1", "u2", "a1", "d0", "d2"),
    "in1": ("a2", "o", "b1", "a0"),
    "in2": ("u2", "o", "u0", "u1", "a2"),
    "sums": ("a0", "s", "b1", "b0", "u0", "b2", "a1"),
    "back0": ("s", "a0", "o"),
    "back1": ("b0", "a1", "a2"),
    "coef": ("b1",),
    "mix0": ("b2", "a2"),
    "mix1": (),
    "mix2": ("s",),
    "end": ("b0", "a1"),
}


def layer_kernel(
    place,
    heads,
    span,
    scale,
    flag,
    centres,
    widths,
    gain_one,
    shift_one,
    gain_two,
    shift_two,
    tokens_h,
    coeffs_h,
    dy_h,
    w_qkv_h,
    w_out_h,
    w_up_h,
    w_down_h,
    mixed_o,
    gtok_o,
    gcoef_o,
    s_qkv_o,
    s_out_o,
    s_up_o,
    s_down_o,
    small_o,
    after_o,
    coeffs,
    dy,
    w_slot,
    w_down,
    x,
    g,
    h1,
    qkv,
    aux,
    joined,
    h2,
    act,
    slope,
    da,
    gcoef,
    acc_a,
    acc_b,
    norms,
    sig,
    k_dup,
    v_dup,
    v_rows,
    weights_e,
    mem_keep,
    s_qkv,
    s_out,
    s_up,
    s_down,
    own_d,
    recv_d,
    own_u0,
    own_u1,
    own_u2,
    recv_u0,
    recv_u1,
    recv_u2,
    own_o,
    recv_o,
    recv_b,
    mem_own,
    mem_recv,
    small_own,
    small_recv,
    load_sem,
    put_sem,
    send_sem,
    recv_sem,
    ready_sem,
    mem_sem,
):
    seq, width = dy.shape
    ff = act.shape[0]
    hd = width // heads
    chunks = seq // LANES
    r, r_d = width // GROUP, ff // GROUP
    third = width // 3
    place.here()
    me = place.me_basis
    loads, puts = {}, []

    def load(name, src, dst):
        loads[name] = pltpu.make_async_copy(src, dst, load_sem.at[len(loads)])
        loads[name].start()

    def put(src, dst):
        copy = pltpu.make_async_copy(src, dst, put_sem.at[len(puts)])
        copy.start()
        puts.append(copy)
        return copy

    slot_qkv, slot_out = w_slot.at[:, pl.ds(0, 3 * width)], w_slot.at[:, pl.ds(3 * width, width)]
    load("tokens", tokens_h, dy)
    load("coeffs", coeffs_h, coeffs)
    load("w_qkv", w_qkv_h, slot_qkv)
    place.greet()
    load("w_out", w_out_h, slot_out)
    load("w_down", w_down_h, w_down)

    given = [ref[...].reshape(1, width) for ref in (gain_one, shift_one, gain_two, shift_two)]
    norms[...] = jnp.transpose(jnp.concatenate(given + [jnp.zeros((LANES - 4, width), f32)], axis=0))

    local = coeffs.shape[1]
    place_of = me * local + lax.broadcasted_iota(jnp.int32, (MEM, local), 1)
    near = lax.broadcasted_iota(jnp.int32, (16, LANES), 0) == lax.broadcasted_iota(jnp.int32, (16, LANES), 1)

    def upright(ref, s):
        parts = []
        for b in range(2):
            row = jnp.concatenate([ref[s, b : b + 1, :], jnp.zeros((1, LANES - heads), jnp.int32)], axis=1).astype(f32)
            parts.append(jnp.sum(jnp.where(near, row, 0.0), axis=1, keepdims=True))
        return jnp.concatenate(parts, axis=0)

    row_id = lax.broadcasted_iota(jnp.int32, (MEM, local), 0)
    real = lax.rem(row_id, 16) < heads
    for s in range(2):
        c, w = upright(centres, s), upright(widths, s)
        spread = w * w + 4.0
        gap = c - place_of.astype(f32)
        value = 2.0 * lax.rsqrt(spread) * jnp.exp(-gap * gap / (2.0 * spread))
        weights_e[s] = jnp.where(real, value, 0.0).astype(bf16)
    loads["coeffs"].wait()
    mem_own[0] = nn(weights_e[1 - me], coeffs[1 - me]).astype(bf16)
    place.greeted()

    def to_beside(i):
        copy = pltpu.make_async_remote_copy(
            src_ref=mem_own.at[i],
            dst_ref=mem_recv.at[i],
            send_sem=mem_sem.at[i, 0],
            recv_sem=mem_sem.at[i, 1],
            device_id=place.beside(),
            device_id_type=MESH,
        )
        copy.start()
        return copy

    samples = to_beside(0)
    mem_keep[...] = nn(weights_e[me], coeffs[me])

    loads["tokens"].wait()

    def enter(c, carry):
        at = lanes_of(c)
        v = jnp.transpose(dy[at, :].astype(f32))
        x[:, at] = v
        n, _ = norm_stats(v)
        h1[:, at] = (n * norms[:, 0 : 1] + norms[:, 1 : 2]).astype(bf16)
        return carry

    lax.fori_loop(0, chunks, enter, 0, unroll=True)
    load("dy", dy_h, dy)
    loads["w_qkv"].wait()
    half_w = width // 2
    for i in range(2):
        at = i * half_w
        qkv[at : at + half_w, :seq] = tn(slot_qkv[:, at : at + half_w], h1[:, :seq]).astype(bf16)
    samples.wait()
    memory = (mem_keep[...] + mem_recv[0].astype(f32)).astype(bf16).astype(f32)
    memory = jnp.concatenate([memory, jnp.zeros((LANES - MEM, width), f32)], axis=0)
    h1[:, seq:] = jnp.transpose(memory).astype(bf16)

    def project(i):
        at = (i + 2) * half_w
        return tn(slot_qkv[:, at : at + half_w], h1[...])

    def keep_projected(i, value):
        at = (i + 2) * half_w
        qkv[at : at + half_w, :] = value.astype(bf16)

    ahead(4, project, keep_projected)
    load("w_up_a", w_up_h.at[:, pl.ds(0, 3 * width)], slot_qkv)
    on = flag[0].astype(f32)
    own_column = own_head((width, LANES), 1, 0, hd)
    mem_part = pl.ds(seq, LANES)
    in_block = lax.broadcasted_iota(jnp.int32, (MEM, seq), 0) // 16 == lax.broadcasted_iota(jnp.int32, (MEM, seq), 1) // span
    for i, dup, rows in ((1, k_dup, None), (2, v_dup, v_rows)):
        wide = jnp.where(own_column, qkv[i * width : (i + 1) * width, mem_part].astype(f32), 0.0)
        dup[...] = (wide + pltpu.roll(wide, MEM, 1)).astype(bf16)
        turned = jnp.transpose(wide)[:MEM]
        if rows is None:
            score = nn((turned * scale).astype(bf16), qkv[:width, :seq])
        else:
            rows[...] = turned.astype(bf16)
    sig[...] = jnp.where(in_block, jax.nn.sigmoid(score), 0.0)
    g[...] = nn(v_dup[...], two_parts(sig[...] * on))

    def heads_forward(i, carry):
        def scores(j):
            h = i * FORWARD_HEADS + j
            base = pl.multiple_of(h * hd, hd)
            q = qkv[pl.ds(base, hd), :seq] * jnp.asarray(scale, bf16)
            k = jnp.transpose(qkv[pl.ds(width + base, hd), :seq])
            return h, base, [nn(k[: first + n], q[:, first : first + n]) for first, n in query_blocks(seq)]

        def use(j, given):
            h, base, products = given
            weights, totals, logs = [], [], []
            for (first, n), s in zip(query_blocks(seq), products):
                s = causal(s, first)
                peak = jnp.max(s, axis=0, keepdims=True)
                e = jnp.exp(s - peak)
                weights.append(e.astype(bf16))
                totals.append(jnp.sum(e, axis=0, keepdims=True))
                logs.append(peak + jnp.log(totals[-1]))
            v = qkv[pl.ds(2 * width + base, hd), :seq]
            o = [nn(v[:, : e.shape[0]], e) / total for e, total in zip(weights, totals)]
            joined[pl.ds(base, hd), :] = (jnp.concatenate(o, axis=1) + g[pl.ds(base, hd), :]).astype(bf16)
            aux[h] = jnp.broadcast_to(jnp.concatenate(logs, axis=1), (8, seq))

        ahead(FORWARD_HEADS, scores, use)
        return carry

    lax.fori_loop(0, heads // FORWARD_HEADS, heads_forward, 0)
    loads["w_out"].wait()
    x[...] = x[...] + tn(slot_out[...], joined[...])
    load("w_up_b", w_up_h.at[:, pl.ds(3 * width, width)], slot_out)
    after_put = put(x, after_o)

    def second(c, carry):
        at = lanes_of(c)
        n, _ = norm_stats(x[:, at])
        h2[:, at] = (n * norms[:, 2 : 3] + norms[:, 3 : 4]).astype(bf16)
        return carry

    lax.fori_loop(0, chunks, second, 0, unroll=True)
    loads["w_up_a"].wait()
    step = 384

    def up_product(i):
        if i * step == 3 * width:
            loads["w_up_b"].wait()
        return tn(w_slot[:, i * step : (i + 1) * step], h2[...])

    def up_use(i, pre):
        sq = pre * pre
        c = math.sqrt(2.0 / math.pi)
        t = jnp.tanh(pre * (c + (c * 0.044715) * sq))
        half = 0.5 + 0.5 * t
        act[i * step : (i + 1) * step, :] = (pre * half).astype(bf16)
        rate = half + (0.5 * pre) * (1.0 - t * t) * (c + (3 * c * 0.044715) * sq)
        slope[i * step // r_d : (i + 1) * step // r_d] = rate.astype(bf16).reshape(step // r_d, r_d, seq)

    ahead(ff // step, up_product, up_use)

    half_d = r_d // 2
    all_shares = {}
    rows_o, columns_o = own_o.shape[1:]
    rows_d, columns_d = own_d.shape[2:]
    own_u, recv_u = (own_u0, own_u1, own_u2), (recv_u0, recv_u1, recv_u2)
    heads_a = heads * 2 // 3
    cols_a, cols_b = heads_a * hd, (heads - heads_a) * hd
    a, b = cols_a // 2, cols_b // 2

    def share(name, p, *where, orders=ORDERS, **more):
        i = len(all_shares)
        all_shares[name] = Share(place, orders[p], *where, send_sem.at[i], recv_sem.at[i], **more)

    for p in range(3):
        share(f"d{p}", p, (own_d.at[p], 0, 0), (recv_d.at[p], 0, 0), rows_d, columns_d, ready_sem=ready_sem.at[p])
    for p in range(3):
        share(f"u{p}", p, (own_u[p], 0, 0), (recv_u[p], 0, 0), *own_u[p].shape[1:])
    share("o", 1, (own_o, 0, 0), (recv_o, 0, 0), rows_o, columns_o)
    spots = {"a": ((0, 0), (0, a), (rows_o, 0)), "b": ((0, 2 * a), (rows_o, a), (rows_o, a + b))}
    for p in range(3):
        before = all_shares[f"d{p}"]
        share(f"a{p}", p, (slope, *spots["a"][p]), (recv_d.at[p], 0, 0), rows_o, a, before=before)
    for p in range(3):
        share(f"b{p}", p, (slope, *spots["b"][p]), (recv_b.at[p], 0, 0), rows_o, b, orders=LATE_ORDERS)
    small = Whole(place, SMALL_ORDER, small_own, small_recv, send_sem.at[13], recv_sem.at[13])
    all_shares["s"] = small

    def pump(names):
        for name in names:
            all_shares[name].pump()
            if name[0] == "d" and all_shares[name].done():
                v, p = all_shares[name].last(), int(name[1])
                s_down[:half_d, p * third : (p + 1) * third] = v[:, :third]
                s_down[half_d:, p * third : (p + 1) * third] = v[:, third:]

    loads["dy"].wait()
    blocks = GROUP // 4

    def down_product(i):
        p, piece = i // 4, i % 4
        return nn(act[piece * blocks * r_d : (piece + 1) * blocks * r_d, :], dy[:, p * third : (p + 1) * third])

    def down_use(i, val):
        p, piece = i // 4, i % 4
        for j in range(blocks):
            v = val[j * r_d : (j + 1) * r_d]
            all_shares[f"d{p}"].store(piece * blocks + j, jnp.concatenate([v[:half_d], v[half_d:]], axis=1))
        if piece == 3:
            all_shares[f"d{p}"].send()
            pump(PLAN[f"down{p}"])

    ahead(12, down_product, down_use)
    loads["w_down"].wait()

    def pre_product(i):
        return nt(w_down[i * step : (i + 1) * step, :], dy[...])

    def pre_use(i, val):
        at = slice(i * step // r_d, (i + 1) * step // r_d)
        rate = slope[at].reshape(step, seq).astype(f32)
        slope[at] = (val * rate).astype(bf16).reshape(step // r_d, r_d, seq)
        if i % 2 == 1:
            pump(PLAN[f"pre{i // 2}"])

    ahead(ff // step, pre_product, pre_use)
    half_up = ff // 2

    def slope_rows(first, count):
        low, high = first // r_d, -(-(first + count) // r_d)
        rows = slope[low:high].reshape((high - low) * r_d, seq)
        return rows[first - low * r_d : first - low * r_d + count]

    pieces, at = [], 0
    for p in range(3):
        part = own_u[p].shape[2]
        for sub in range(0, part, 256):
            count = min(256, part - sub)
            pieces.append((p, sub, at, count, sub + count == part))
            at += count

    def up_grad(i):
        _, _, at, count, _ = pieces[i]
        return nt(h2[...], slope_rows(at, count)), nt(h2[...], slope_rows(half_up + at, count))

    def up_grad_use(i, val):
        (p, sub, _, _, ends), (left, right) = pieces[i], val
        for j in range(GROUP):
            rows = slice(j * r, (j + 1) * r)
            all_shares[f"u{p}"].store(j, jnp.concatenate([left[rows], right[rows]], axis=0), sub)
        if ends:
            all_shares[f"u{p}"].send()
            pump(PLAN[f"up{p}"])

    ahead(len(pieces), up_grad, up_grad_use)
    for i in range(3):
        rows = slice(i * third, (i + 1) * third)
        g[rows, :] = nn(w_slot[rows, :], slope[...].reshape(ff, seq))
        pump(PLAN[f"hid{i}"])
    load("w_qkv2", w_qkv_h, slot_qkv)
    load("w_out2", w_out_h, slot_out)

    acc_b[...] = jnp.zeros_like(acc_b)
    acc_a[...] = jnp.zeros_like(acc_a)

    def second_back(c, carry):
        at = lanes_of(c)
        n, inv = norm_stats(x[:, at])
        u = g[:, at]
        un = u * n
        acc_b[...] += un
        acc_a[...] += u
        ug = u * norms[:, 2 : 3]
        m1 = jnp.mean(ug, axis=0, keepdims=True)
        m2 = jnp.mean(un * norms[:, 2 : 3], axis=0, keepdims=True)
        v = jnp.transpose(dy[at, :].astype(f32)) + inv * (ug - m1 - n * m2)
        g[:, at] = v
        da[:, at] = v.astype(bf16)
        return carry

    lax.fori_loop(0, chunks, second_back, 0, unroll=True)
    load("tokens2", tokens_h, dy)
    small_own[0, 2:3, :] = columns_sum(acc_b)
    small_own[0, 3:4, :] = columns_sum(acc_a)
    small_own[0, 4:8, :] = jnp.zeros((4, width), f32)
    pump(PLAN["norm2"])
    half_o = width // 2
    left, right = nt(joined[...], da[:half_o, :]), nt(joined[...], da[half_o:, :])
    for j in range(GROUP):
        rows = slice(j * r, (j + 1) * r)
        all_shares["o"].store(j, jnp.concatenate([left[rows], right[rows]], axis=0))
    all_shares["o"].send()
    pump(PLAN["out"])
    loads["w_out2"].wait()
    datt = h2
    datt[...] = nn(slot_out[...], da[...]).astype(bf16)
    pump(PLAN["att"])

    gates = sig[...]
    dscore = two_parts((on * scale) * nn(v_rows[...], datt[...]) * gates * (1.0 - gates))
    after_put.wait()
    x[...] = nn(k_dup[...], dscore)
    for i, wide in ((1, nt(qkv[:width, :seq], dscore)), (2, nt(datt[...], two_parts(gates * on)))):
        total = wide + pltpu.roll(wide, LANES - MEM, 1)
        qkv[i * width : (i + 1) * width, mem_part] = jnp.where(own_column, total, 0.0).astype(bf16)
    qkv[:width, mem_part] = jnp.zeros((width, LANES), bf16)

    def pair_back(i):
        todo = []
        for h in (2 * i, 2 * i + 1):
            at_q, at_k, at_v = (slice(j * width + h * hd, j * width + (h + 1) * hd) for j in range(3))
            q = qkv[at_q, :seq] * jnp.asarray(scale, bf16)
            k = qkv[at_k, :seq]
            k_up, v_up = jnp.transpose(k), jnp.transpose(qkv[at_v, :seq])
            do = datt[at_q, :]
            s = [nn(k_up[: first + n], q[:, first : first + n]) for first, n in query_blocks(seq)]
            dp = [nn(v_up[: first + n], do[:, first : first + n]) for first, n in query_blocks(seq)]
            todo.append((h, at_q, at_k, at_v, q, k * jnp.asarray(scale, bf16), do, s, dp))
        ready = []
        for h, at_q, at_k, at_v, q, k, do, scores, grads in todo:
            log_total = aux[h, 0:1, :]
            ps, dss = [], []
            for (first, n), s, dp in zip(query_blocks(seq), scores, grads):
                p = jnp.exp(causal(s, first) - log_total[:, first : first + n])
                ps.append(p.astype(bf16))
                dss.append((p * (dp - jnp.sum(p * dp, axis=0, keepdims=True))).astype(bf16))
            ready.append((ps, dss))
        for (h, at_q, at_k, at_v, q, k, do, _, _), (ps, dss) in zip(todo, ready):
            dq, dk, dv = [], [], []
            for (first, n), p, ds in zip(query_blocks(seq), ps, dss):
                dq.append(nn(k[:, : first + n], ds))
                dk.append(nt(q[:, first : first + n], ds))
                dv.append(nt(do[:, first : first + n], p))
            qkv[at_q, :seq] = (jnp.concatenate(dq, axis=1) + x[at_q, :]).astype(bf16)
            qkv[at_k, :seq] = add_up(dk).astype(bf16)
            qkv[at_v, :seq] = add_up(dv).astype(bf16)

    def grad_qkv(name, first, count):
        def product(p):
            at = p * width + first
            return nt(h1[...], qkv[at : at + count, :])

        def use(p, val):
            for j in range(GROUP):
                v = val[j * r : (j + 1) * r]
                all_shares[f"{name}{p}"].store(j, jnp.concatenate([v[:, : count // 2], v[:, count // 2 :]], axis=0))
            all_shares[f"{name}{p}"].send()
            pump(PLAN[f"{name}{p}"])

        if name == "b":
            ahead(3, product, use)
        else:
            for p in range(3):
                use(p, product(p))

    pairs = heads // 2
    for i in range(pairs):
        pair_back(i)
        pump(PLAN[f"pair{i}"])
        if 2 * (i + 1) == heads_a:
            grad_qkv("a", 0, cols_a)
    grad_qkv("b", cols_a, cols_b)

    loads["tokens2"].wait()
    loads["w_qkv2"].wait()
    gm = []
    for i in range(3):
        rows = slice(i * third, (i + 1) * third)
        val = nn(slot_qkv[rows, :], qkv[...])
        x[rows, :] = val[:, :seq]
        gm.append(val[:, seq:])
        pump(PLAN[f"in{i}"])
    mem_own[1] = jnp.transpose(jnp.concatenate(gm, axis=0))[:MEM].astype(bf16)
    grads = to_beside(1)
    acc_b[...] = jnp.zeros_like(acc_b)
    acc_a[...] = jnp.zeros_like(acc_a)

    def first_sums(c, carry):
        at = lanes_of(c)
        n, inv = norm_stats(jnp.transpose(dy[at, :].astype(f32)))
        u = x[:, at]
        un = u * n
        acc_b[...] += un
        acc_a[...] += u
        joined[:, at] = n.astype(bf16)
        m1 = jnp.mean(u * norms[:, 0:1], axis=0, keepdims=True)
        m2 = jnp.mean(un * norms[:, 0:1], axis=0, keepdims=True)
        sig[0:8, at] = jnp.concatenate([inv, m1, m2, jnp.zeros((5, LANES), f32)], axis=0)
        return carry

    lax.fori_loop(0, chunks, first_sums, 0, unroll=True)
    small_own[0, 0:1, :] = columns_sum(acc_b)
    small_own[0, 1:2, :] = columns_sum(acc_a)
    small.send()
    pump(PLAN["sums"])

    def first_back(c, carry):
        at = lanes_of(c)
        inv, m1, m2 = sig[0:1, at], sig[1:2, at], sig[2:3, at]
        n = joined[:, at].astype(f32)
        g[:, at] = g[:, at] + inv * (x[:, at] * norms[:, 0:1] - m1 - n * m2)
        return carry

    lax.fori_loop(0, 3, first_back, 0, unroll=True)
    pump(PLAN["back0"])
    lax.fori_loop(3, chunks, first_back, 0, unroll=True)
    put(g, gtok_o)
    load("after", after_o, x)
    pump(PLAN["back1"])
    grads.wait()
    gcoef[me] = tn(weights_e[me], mem_own[1])
    gcoef[1 - me] = tn(weights_e[1 - me], mem_recv[1])
    put(gcoef, gcoef_o)
    pump(PLAN["coef"])
    loads["after"].wait()
    for i in range(3):
        cols = slice(i * third, (i + 1) * third)
        dy[:, cols] = jnp.transpose(x[cols, :] + tn(w_down[:, cols], act[...])).astype(bf16)
        pump(PLAN[f"mix{i}"])
    put(dy, mixed_o)
    put(s_down, s_down_o)
    pump(PLAN["end"])
    at = 0
    for p in range(3):
        part = own_u[p].shape[2]
        v = all_shares[f"u{p}"].last()
        s_up[:, at : at + part] = v[:r]
        s_up[:, half_up + at : half_up + at + part] = v[r:]
        at += part
    put(s_up, s_up_o)
    v = all_shares["o"].last()
    s_out[:, :half_o] = v[:r]
    s_out[:, half_o:] = v[r:]
    put(s_out, s_out_o)
    for p in range(3):
        for name, first, count in (("a", 0, cols_a), ("b", cols_a, cols_b)):
            at = p * width + first
            v = all_shares[f"{name}{p}"].last()
            s_qkv[:, at : at + count // 2] = v[:r]
            s_qkv[:, at + count // 2 : at + count] = v[r:]
    put(s_qkv, s_qkv_o)
    put(small_own.at[len(SMALL_ORDER)], small_o)
    for copy in puts:
        if copy is not after_put:
            copy.wait()


def run_layer(place, heads, blocks, flag, centres, widths, norms, tokens, coeffs, dy, w_qkv, w_out, w_up, w_down):
    seq, width = tokens.shape
    ff = w_up.shape[1]
    local = coeffs.shape[1]
    span = seq // blocks
    scale = 1.0 / math.sqrt(width // heads)
    r, r_d = width // GROUP, ff // GROUP
    wide = seq + LANES
    S = jax.ShapeDtypeStruct
    outs = [
        S((seq, width), bf16),
        S((width, seq), f32),
        S((2, local, width), f32),
        S((r, 3 * width), f32),
        S((r, width), f32),
        S((r, ff), f32),
        S((r_d, width), f32),
        S((8, width), f32),
        S((width, seq), f32),
    ]
    part_d = (r_d // 2, 2 * width // 3)
    unit = ff // 24
    parts_u = [(2 * r, n * unit) for n in (5, 4, 3)]
    part_o = (2 * r, width // 2)

    def vm(*shape, dtype=bf16):
        return pltpu.VMEM(shape, dtype)

    scratch = [
        vm(2, local, width),
        vm(seq, width),
        vm(width, ff),
        vm(ff, width),
        vm(width, seq, dtype=f32),
        vm(width, seq, dtype=f32),
        vm(width, wide),
        vm(3 * width, wide),
        vm(heads, 8, seq, dtype=f32),
        vm(width, seq),
        vm(width, seq),
        vm(ff, seq),
        vm(GROUP, r_d, seq),
        vm(width, seq),
        vm(2, local, width, dtype=f32),
        vm(width, LANES, dtype=f32),
        vm(width, LANES, dtype=f32),
        vm(width, LANES, dtype=f32),
        vm(MEM, seq, dtype=f32),
        vm(width, LANES),
        vm(width, LANES),
        vm(MEM, width),
        vm(2, MEM, local),
        vm(MEM, width, dtype=f32),
        vm(r, 3 * width, dtype=f32),
        vm(r, width, dtype=f32),
        vm(r, ff, dtype=f32),
        vm(r_d, width, dtype=f32),
        vm(3, GROUP, *part_d),
        vm(3, GROUP - 1, *part_d),
        *[vm(GROUP, *part) for part in parts_u],
        *[vm(GROUP - 1, *part) for part in parts_u],
        vm(GROUP, *part_o),
        vm(GROUP - 1, *part_o),
        vm(3, GROUP - 1, 2 * r, width // 6),
        vm(2, MEM, width),
        vm(2, MEM, width),
        vm(len(SMALL_ORDER) + 1, 8, width, dtype=f32),
        vm(len(PARTNERS), 8, width, dtype=f32),
        pltpu.SemaphoreType.DMA((12,)),
        pltpu.SemaphoreType.DMA((9,)),
        pltpu.SemaphoreType.DMA((14, len(PARTNERS))),
        pltpu.SemaphoreType.DMA((14, len(PARTNERS))),
        pltpu.SemaphoreType.REGULAR((3, STAGES)),
        pltpu.SemaphoreType.DMA((2, 2)),
    ]
    return pl.pallas_call(
        functools.partial(layer_kernel, place, heads, span, scale),
        out_shape=outs,
        in_specs=[SM] + [VM] * 6 + [ANY] * 7,
        out_specs=[ANY] * len(outs),
        scratch_shapes=scratch,
        compiler_params=pltpu.CompilerParams(vmem_limit_bytes=VMEM_MIB * 2**20, collective_id=0, has_side_effects=True),
    )(flag, centres, widths, *norms, tokens, coeffs, dy, w_qkv, w_out, w_up, w_down)


def hand_on(place, mixed, gtok, small, *arrays):
    width = small.shape[1]
    part = width // (place.dp * place.basis)
    count = 3 + len(arrays)

    def kernel(*refs):
        ins, outs, vectors = refs[:count], refs[count : 2 * count - 1], refs[2 * count - 1 : 2 * count + 3]
        held, parts = refs[2 * count + 3 : 3 * count + 3], refs[3 * count + 3 : 3 * count + 7]
        upright, in_sem, out_sem = refs[3 * count + 7 :]
        coming = [pltpu.make_async_copy(ins[i], held[i], in_sem.at[i]) for i in range(count)]
        leaving = []

        def leave(src, dst):
            leaving.append(pltpu.make_async_copy(src, dst, out_sem.at[len(leaving)]))
            leaving[-1].start()

        for copy in coming:
            copy.start()
        coming[0].wait()
        for c in range(gtok.shape[1] // LANES):
            at = slice(c * LANES, (c + 1) * LANES)
            upright[at, :] = jnp.transpose(held[0][:, at])
            leave(upright.at[at, :], outs[0].at[at, :])
        for i in range(1, count - 1):
            coming[i].wait()
            leave(held[i], outs[i])
        coming[-1].wait()
        flat = lax.axis_index("dp") * place.basis + lax.axis_index("basis")
        turned = pltpu.roll(held[-1][...], lax.rem(width - flat * part, width), 1)
        for i in range(4):
            parts[i][...] = turned[i, :part]
            leave(parts[i], vectors[i])
        for copy in leaving:
            copy.wait()

    S = jax.ShapeDtypeStruct
    arrays = (gtok, mixed, *arrays, small)
    shapes = [S(gtok.shape[::-1], f32)] + [S(a.shape, a.dtype) for a in arrays[1:-1]]
    return pl.pallas_call(
        kernel,
        out_shape=shapes + [S((part,), f32)] * 4,
        in_specs=[ANY] * count,
        out_specs=[ANY] * (count + 3),
        scratch_shapes=[pltpu.VMEM(a.shape, a.dtype) for a in arrays]
        + [pltpu.VMEM((part,), f32)] * 4
        + [pltpu.VMEM(gtok.shape[::-1], f32)]
        + [pltpu.SemaphoreType.DMA((count,)), pltpu.SemaphoreType.DMA((count + 2 + gtok.shape[1] // LANES,))],
        compiler_params=pltpu.CompilerParams(vmem_limit_bytes=VMEM_MIB * 2**20),
    )(*arrays)


def halve_rest(place, rows):
    for bit in reversed(range(place.low)):
        half = rows.shape[0] // 2
        if bit < place.basis_bits:
            axis, size, mask = "basis", place.basis, 1 << bit
        else:
            axis, size, mask = "dp", place.dp, 1 << (bit - place.basis_bits)
        mine = (lax.axis_index(axis) // mask) % 2
        keep = lax.dynamic_slice_in_dim(rows, mine * half, half, 0)
        give = lax.dynamic_slice_in_dim(rows, (1 - mine) * half, half, 0)
        rows = keep + lax.ppermute(give, axis, [(i, i ^ mask) for i in range(size)])
    return rows


def sum_rest(place, values):
    for bit in range(place.low):
        if bit < place.basis_bits:
            axis, size, mask = "basis", place.basis, 1 << bit
        else:
            axis, size, mask = "dp", place.dp, 1 << (bit - place.basis_bits)
        values = values + lax.ppermute(values, axis, [(i, i ^ mask) for i in range(size)])
    return values


def on_device(
    place,
    tokens,
    w_qkv,
    w_out,
    w_up,
    w_down,
    gain_one,
    shift_one,
    gain_two,
    shift_two,
    coeffs,
    flags,
    centres,
    widths,
    cotangent,
):
    width = tokens.shape[2]
    heads, blocks = centres.shape[1], centres.shape[2]
    norms = [gain_one, shift_one, gain_two, shift_two]
    turned = [jnp.transpose(v, (0, 2, 1)) for v in (centres, widths)]
    mixed, gtok, gcoef, *shares, small, _ = run_layer(
        place, heads, blocks, flags, *turned, norms, tokens[0], coeffs, cotangent[0], w_qkv, w_out, w_up, w_down
    )
    small = sum_rest(place, small)
    gtok, mixed, gcoef, s_qkv, s_out, s_up, s_down, *vectors = hand_on(place, mixed, gtok, small, gcoef, *shares)
    shares = [halve_rest(place, s) for s in (s_qkv, s_out, s_up, s_down)]
    return (mixed[None], gtok[None], gcoef, *shares, *vectors)


def solution(mesh):
    both = ("dp", "basis")
    held = P(both, None, None)
    memory = P("dp", None, None)
    in_specs = (held,) + (P(),) * 8 + (P("dp", "basis", None), P(both), memory, memory, held)
    out_specs = (held, held, P("dp", "basis", None)) + (P(both, None),) * 4 + (P(both),) * 4
    return jax.shard_map(
        functools.partial(on_device, Place(mesh.shape)), mesh=mesh, in_specs=in_specs, out_specs=out_specs, check_vma=False
    )
```
